512 devices in a mesh: dp: 8 (over z), ctx: 64 (over y, x, core).
Axes of the slice: x: 4, y: 8, z: 8, core: 2. Of those that a mesh axis runs over, the one named last changes fastest.
Arguments:
- query_act: bfloat16 [8, 8192, 2048], P('dp', 'ctx'), may hold values from -6 to 6
- key_act: bfloat16 [8, 8192, 2048], P('dp', 'ctx'), may hold values from -6 to 6
- value_act: bfloat16 [8, 8192, 2048], P('dp', 'ctx'), may hold values from -6 to 6
- grad_out: bfloat16 [8, 8192, 2048], P('dp', 'ctx'), may hold values from -16 to 16
- filter_taps: bfloat16 [128, 2048], replicated, may hold values from -2.5 to 2.5
Outputs:
- output_act: bfloat16 [8, 8192, 2048], P('dp', 'ctx')
- grad_query: bfloat16 [8, 8192, 2048], P('dp', 'ctx')
- grad_key: bfloat16 [8, 8192, 2048], P('dp', 'ctx')
- grad_value: bfloat16 [8, 8192, 2048], P('dp', 'ctx')
- grad_filter: float32 [128, 2048], P(None, 'ctx')
The draws below stay inside these ranges and needn't reach their ends.
All inputs are finite; a program needn't handle non-finite values.
Results may differ from the reference program's by a relative error of at most 0.0065.
Values may be sent and summed in bfloat16 or wider, within the bound.
A program may use at most 64 MiB of HBM per device.

```python
import math
import jax
import jax.numpy as jnp
from jax import lax

C = 2048
LH = 128
SEQS = 8
LEN = 8192


def draw_filter_taps(key, part):
    key = jax.random.fold_in(key, 7)
    rate_key, noise_key = jax.random.split(key, 2)
    horizon = jnp.exp(jax.random.uniform(rate_key, (C,), jnp.float32, math.log(8.0), math.log(600.0)))
    rough_part = jnp.clip(jax.random.normal(noise_key, (LH, C), jnp.float32), -4.0, 4.0)
    tap_index = jnp.arange(LH, dtype=jnp.float32)[:, None]
    falloff = jnp.exp(-tap_index / horizon[None, :])
    amplitude = 1.5 / jnp.sqrt(jnp.minimum(float(LH), horizon / 2.0) + 1.0)
    return jnp.clip(rough_part * falloff * amplitude[None, :], -2.5, 2.5).astype(jnp.bfloat16)


def raised(entries, stream_key, source, target, parts, factor):
    def block_of(position):
        return (jnp.arange(entries.shape[position]) // (entries.shape[position] // parts)).reshape((-1,) + (1,) * (entries.ndim - 1 - position))

    first = jax.random.permutation(stream_key, parts)[block_of(target)]
    second = (block_of(target) + parts // 2) % parts
    return jnp.where((block_of(source) == first) | (block_of(source) == second), factor * entries, entries)


def block_levels(key, dims, cuts, least, top_value):
    gain, own = 1.0, jax.random.fold_in(key, 6)
    for axis_at, parts in cuts:
        draws = jnp.exp(jax.random.uniform(jax.random.fold_in(own, axis_at), (parts,), jnp.float32, least / len(cuts), top_value / len(cuts)))
        gain = gain * jnp.repeat(draws, dims[axis_at] // parts).reshape([-1 if axis == axis_at else 1 for axis in range(len(dims))])
    return gain


def bell_draw(key, extent, width, limit, pieces=(), held_as=jnp.bfloat16):
    values = width * jax.random.normal(key, extent, jnp.float32)
    if pieces:
        values = values * block_levels(key, extent, pieces, -0.22, 0.18)
    return jnp.clip(values, -limit, limit).astype(held_as)


def heavy_noise(stream_key, extent, deviation, reach, cuts, heavy, held_as=jnp.bfloat16):
    values = deviation * jax.random.normal(stream_key, extent, jnp.float32)
    if cuts:
        values = values * block_levels(stream_key, extent, cuts, -0.22, 0.18)
    return jnp.clip(raised(values, jax.random.fold_in(stream_key, 3), *heavy), -reach, reach).astype(held_as)


def setup_inputs(seed: int = 0) -> dict:
    keys = jax.random.split(jax.random.key(seed), 6)
    query_act = bell_draw(keys[0], (SEQS, LEN, C), 1.0, 6.0, ((0, 8), (1, 64)))
    key_act = bell_draw(keys[1], (SEQS, LEN, C), 1.0, 6.0, ((0, 8), (1, 64)))
    value_act = bell_draw(keys[2], (SEQS, LEN, C), 1.0, 6.0, ((0, 8), (1, 64)))
    grad_out = heavy_noise(keys[3], (SEQS, LEN, C), 1.0, 16.0, ((0, 8), (1, 64)), (1, 2, 64, 4.0))
    filter_taps = draw_filter_taps(jax.random.fold_in(keys[5], 71), 0)
    return dict(query_act=query_act, key_act=key_act, value_act=value_act, grad_out=grad_out, filter_taps=filter_taps)


def fft_conv(first_arr, second_arr, size_fft):
    spectrum = jnp.fft.rfft(first_arr, size_fft, axis=0) * jnp.fft.rfft(second_arr, size_fft, axis=0)
    return jnp.fft.irfft(spectrum, size_fft, axis=0)

def reference(query_act, key_act, value_act, grad_out, filter_taps):
    weights = filter_taps.astype(jnp.float32)
    size_fft = 2 * LEN

    def one_sequence(items):
        query_rows, key_rows, value_rows, grad_rows = items
        query_f = query_rows.astype(jnp.float32)
        key_f = key_rows.astype(jnp.float32)
        value_f = value_rows.astype(jnp.float32)
        grad_f = grad_rows.astype(jnp.float32)
        kv_product = (key_f * value_f).astype(jnp.bfloat16).astype(jnp.float32)
        filtered = fft_conv(kv_product, weights, size_fft)[:LEN]
        output_rows = (query_f * filtered).astype(jnp.bfloat16)
        grad_query_rows = (grad_f * filtered).astype(jnp.bfloat16)
        gate_grad = (grad_f * query_f).astype(jnp.bfloat16).astype(jnp.float32)
        reversed_grad = gate_grad[::-1]
        flowing = fft_conv(reversed_grad, weights, size_fft)[:LEN][::-1]
        grad_key_rows = (flowing * value_f).astype(jnp.bfloat16)
        grad_value_rows = (flowing * key_f).astype(jnp.bfloat16)
        crossed = fft_conv(reversed_grad, kv_product, size_fft)
        lagged = crossed[LEN - LH:LEN][::-1]
        return (output_rows, grad_query_rows, grad_key_rows, grad_value_rows, lagged)
    outputs = lax.map(one_sequence, (query_act, key_act, value_act, grad_out))
    grad_filter = lax.optimization_barrier(jnp.sum(outputs[4], axis=0)) * (1.0 / math.sqrt(SEQS * LEN))
    return (outputs[0], outputs[1], outputs[2], outputs[3], grad_filter)
```

```python
import functools
import math

import jax
import jax.numpy as jnp
import ml_dtypes
import numpy as np
from jax import lax
from jax.experimental import pallas as pl
from jax.experimental.pallas import tpu as pltpu
from jax.sharding import PartitionSpec as P

MESH = pl.DeviceIdType.MESH
bf16 = jnp.bfloat16
f32 = jnp.float32
T = 128
F = 128
W = 128
NX = 4


def split(matrix):
    hi = matrix.astype(ml_dtypes.bfloat16)
    lo = (matrix - hi.astype(np.float64)).astype(ml_dtypes.bfloat16)
    return hi, lo


def transforms():
    theta = np.pi * (2 * np.arange(F) + 1) / 256.0
    n = np.arange(T)

    def forward(shift):
        angle = theta[:, None] * (n + shift)[None, :]
        return np.concatenate([np.cos(angle), -np.sin(angle)], axis=0)

    own_hi, own_lo = split(forward(0))
    prev_hi, prev_lo = split(forward(-T))
    back_hi, back_lo = split(forward(0).T / F)
    return (
        np.concatenate([own_hi, own_lo], axis=1),
        np.concatenate([prev_hi, prev_lo], axis=1),
        np.concatenate([back_hi, back_hi, back_lo], axis=1),
    )


def kernel(
    nz, ny,
    q_hbm, k_hbm, v_hbm, g_hbm, h_hbm, own_hbm, prev_hbm, back_hbm,
    y_ref, gq_ref, gk_ref, gv_ref, gf_ref,
    q_ref, k_ref, v_ref, g_ref, h_ref, own_ref, prev_ref, back_ref,
    prev_k, prev_g, kg, halo, extra, spec_k, spec_g, spec_h,
    part, recv1, part2, recv2, part3, recv3,
    load_sem, halo_send, halo_recv, late_recv, extra_send, extra_recv,
    send1, sem1, send2, sem2, send3, sem3,
):
    z = lax.axis_index("dp")
    c = lax.axis_index("ctx")
    nc = ny * 2 * NX
    yy = c // (2 * NX)
    x = (c // 2) % NX
    core = c % 2
    near = 1 - core
    right = {"dp": z, "ctx": lax.rem(c + 1, nc)}
    left = {"dp": z, "ctx": lax.rem(c + nc - 1, nc)}
    partner = {"dp": z, "ctx": c + 1 - 2 * core}

    def at_y(d):
        return {"dp": z, "ctx": lax.rem(yy + d, ny) * (2 * NX) + x * 2 + core}

    def at_z(d):
        return {"dp": lax.rem(z + d, nz), "ctx": c}

    def at_x(xs, ks):
        return {"dp": z, "ctx": yy * (2 * NX) + xs * 2 + ks}

    loads = [
        pltpu.make_async_copy(src, dst, load_sem.at[i])
        for i, (src, dst) in enumerate([
            (k_hbm.at[0], k_ref), (v_hbm.at[0], v_ref), (q_hbm.at[0], q_ref), (g_hbm.at[0], g_ref),
            (own_hbm, own_ref), (prev_hbm, prev_ref), (back_hbm, back_ref), (h_hbm, h_ref),
        ])
    ]
    for copy in loads:
        copy.start()

    barrier = pltpu.get_barrier_semaphore()

    def greet(device):
        pl.semaphore_signal(barrier, inc=1, device_id=device, device_id_type=MESH)

    greet(left)
    greet(right)
    for d in range(1, ny):
        greet(at_y(d))
    for d in range(1, nz):
        greet(at_z(d))
    source_core = x // 2
    for xs in range(NX):
        @pl.when(jnp.logical_or(xs != x, source_core != core))
        def _():
            greet(at_x(xs, source_core))

    def columns(s, b):
        return pl.ds(pl.multiple_of(b * (2 * W) + s * W, W), W)

    def products(s):
        def step(b, carry):
            cols = columns(s, b)
            kg[0, s, b] = (k_ref[:, cols].astype(f32) * v_ref[:, cols].astype(f32)).astype(bf16)
            kg[1, s, b] = (g_ref[:, cols].astype(f32) * q_ref[:, cols].astype(f32)).astype(bf16)
            return carry

        lax.fori_loop(0, ny, step, 0)

    for copy in loads[:4]:
        copy.wait()
    products(near)
    targets = jnp.where(source_core == core, 3, 4)
    pl.semaphore_wait(barrier, 2 + (ny - 1) + (nz - 1) + targets)

    def halo_copy(array, s, b, device):
        return pltpu.make_async_remote_copy(
            src_ref=kg.at[array, s, b], dst_ref=halo.at[array, s, b],
            send_sem=halo_send.at[array], recv_sem=halo_recv.at[array, b],
            device_id=device, device_id_type=MESH,
        )

    def late_copy(array, device):
        return pltpu.make_async_remote_copy(
            src_ref=kg.at[array, core], dst_ref=halo.at[array, core],
            send_sem=halo_send.at[array], recv_sem=late_recv.at[array],
            device_id=device, device_id_type=MESH,
        )

    def extra_copy(b):
        return pltpu.make_async_remote_copy(
            src_ref=kg.at[near, near, b], dst_ref=extra.at[b],
            send_sem=extra_send, recv_sem=extra_recv.at[b],
            device_id=partner, device_id_type=MESH,
        )

    def early(i, carry):
        b = lax.rem(yy + 1 + i, ny)
        halo_copy(0, near, b, right).start()
        halo_copy(1, near, b, left).start()
        extra_copy(b).start()
        return carry

    lax.fori_loop(0, ny, early, 0)
    products(core)

    for copy in loads[4:]:
        copy.wait()
    prev_k[...] = prev_ref[...] * jnp.where(c > 0, 1.0, 0.0).astype(bf16)
    prev_g[...] = prev_ref[...] * jnp.where(c < nc - 1, -1.0, 0.0).astype(bf16)

    def twice(value):
        return jnp.concatenate([value, value], axis=0)

    def forward(matrix, value):
        return jnp.dot(matrix, twice(value), preferred_element_type=f32)

    def pair(ref, *index):
        *lead, b0, b1 = index
        return jnp.concatenate([ref[(*lead, b0)], ref[(*lead, b1)]], axis=1)

    def put(ref, s, b0, b1, value):
        ref[s, b0] = value[:, :W]
        ref[s, b1] = value[:, W:]

    def own_spectra(s):
        def step(i, carry):
            b0, b1 = 2 * i, 2 * i + 1
            put(spec_k, s, b0, b1, forward(own_ref[...], pair(kg, 0, s, b0, b1)))
            put(spec_g, s, b0, b1, forward(own_ref[...], pair(kg, 1, s, b0, b1)))
            taps = jnp.concatenate([h_ref[:, columns(s, b0)], h_ref[:, columns(s, b1)]], axis=1)
            put(spec_h, s, b0, b1, forward(own_ref[...], taps))
            return carry

        lax.fori_loop(0, ny // 2, step, 0)

    own_spectra(core)
    own_spectra(near)

    def times(a, b):
        ar, ai, br, bi = a[:F], a[F:], b[:F], b[F:]
        return ar * br - ai * bi, ar * bi + ai * br

    def times_conj(a, b):
        ar, ai, br, bi = a[:F], a[F:], b[:F], b[F:]
        return ar * br + ai * bi, ai * br - ar * bi

    def inverse(re, im):
        value = jnp.concatenate([re, im], axis=0)
        hi = value.astype(bf16)
        lo = (value - hi.astype(f32)).astype(bf16)
        return jnp.dot(
            back_ref[...], jnp.concatenate([hi, lo, hi], axis=0), preferred_element_type=f32
        )

    def gradient(i, carry):
        b0 = lax.rem(yy + 1 + 2 * i, ny)
        b1 = lax.rem(yy + 2 + 2 * i, ny)
        for b in (b0, b1):
            halo_copy(0, core, b, right).wait_recv()
            halo_copy(1, core, b, left).wait_recv()
            extra_copy(b).wait_recv()
        own_k = pair(spec_k, core, b0, b1)
        own_g = pair(spec_g, core, b0, b1)
        k_prev = forward(prev_k[...], pair(halo, 0, core, b0, b1))
        g_next = forward(prev_g[...], pair(halo, 1, core, b0, b1))
        other = forward(prev_ref[...], pair(extra, b0, b1))
        g_all = own_g + g_next
        put(spec_k, core, b0, b1, own_k + k_prev)
        put(spec_g, core, b0, b1, g_all)
        first = core == 0
        u = jnp.where(first, -g_next, other)
        w = jnp.where(first, other, k_prev)
        re0, im0 = times_conj(g_all, own_k)
        re1, im1 = times_conj(own_g, k_prev)
        re2, im2 = times_conj(u, w)
        value = inverse(re0 + re1 + re2, im0 + im1 + im2).astype(bf16)
        part[b0] = value[:, :W]
        part[b1] = value[:, W:]

        def send(d, b):
            pltpu.make_async_remote_copy(
                src_ref=part.at[b], dst_ref=recv1.at[d - 1], send_sem=send1, recv_sem=sem1,
                device_id=at_y(d), device_id_type=MESH,
            ).start()

        send(1 + 2 * i, b0)

        @pl.when(i < ny // 2 - 1)
        def _():
            send(2 + 2 * i, b1)

        return carry

    late_copy(0, right).start()
    late_copy(1, left).start()
    lax.fori_loop(0, ny // 2, gradient, 0)

    def outputs(s):
        def step(i, carry):
            b0, b1 = 2 * i, 2 * i + 1
            k_all = pair(spec_k, s, b0, b1)
            g_all = pair(spec_g, s, b0, b1)
            if s is near:
                k_all += forward(prev_k[...], pair(halo, 0, s, b0, b1))
                g_all += forward(prev_g[...], pair(halo, 1, s, b0, b1))
            taps = pair(spec_h, s, b0, b1)
            mixed = inverse(*times(k_all, taps))
            flowing = inverse(*times_conj(g_all, taps))
            for at, b in enumerate((b0, b1)):
                cols = columns(s, b)
                m = mixed[:, at * W:(at + 1) * W]
                y_ref[0, :, cols] = (q_ref[:, cols].astype(f32) * m).astype(bf16)
                gq_ref[0, :, cols] = (g_ref[:, cols].astype(f32) * m).astype(bf16)
                m = flowing[:, at * W:(at + 1) * W]
                gk_ref[0, :, cols] = (v_ref[:, cols].astype(f32) * m).astype(bf16)
                gv_ref[0, :, cols] = (k_ref[:, cols].astype(f32) * m).astype(bf16)
            return carry

        lax.fori_loop(0, ny // 2, step, 0)

    outputs(core)

    def late_arrival(array, device):
        return pltpu.make_async_remote_copy(
            src_ref=kg.at[array, near], dst_ref=halo.at[array, near],
            send_sem=halo_send.at[array], recv_sem=late_recv.at[array],
            device_id=device, device_id_type=MESH,
        )

    late_arrival(0, right).wait_recv()
    late_arrival(1, left).wait_recv()
    outputs(near)

    def landed(ref, sem):
        pltpu.make_async_copy(ref, ref, sem).wait()

    landed(recv1, sem1)
    total = part[yy].astype(f32)
    for d in range(ny - 1):
        total += recv1[d].astype(f32)
    part2[...] = jnp.transpose(total).astype(bf16).reshape(4, 32, T)
    for r in range(2):
        for ks in range(2):
            xs = 2 * core + r

            @pl.when(jnp.logical_or(xs != x, ks != core))
            def _():
                pltpu.make_async_remote_copy(
                    src_ref=part2.at[r * 2 + ks], dst_ref=recv2.at[x], send_sem=send2, recv_sem=sem2.at[x],
                    device_id=at_x(xs, ks), device_id_type=MESH,
                ).start()

            @pl.when(jnp.logical_not(jnp.logical_or(xs != x, ks != core)))
            def _():
                recv2[x] = part2[r * 2 + ks]
    for xs in range(NX):
        @pl.when(jnp.logical_or(xs != x, source_core != core))
        def _():
            landed(recv2.at[xs], sem2.at[xs])
    total = recv2[0].astype(f32)
    for xs in range(1, NX):
        total += recv2[xs].astype(f32)
    part3[...] = total
    for d in range(1, nz):
        pltpu.make_async_remote_copy(
            src_ref=part3, dst_ref=recv3.at[d - 1], send_sem=send3, recv_sem=sem3,
            device_id=at_z(d), device_id_type=MESH,
        ).start()
    landed(recv3, sem3)
    for d in range(nz - 1):
        total += recv3[d]
    gf_ref[...] = total * (1.0 / math.sqrt(T * nc * nz))

    landed(kg.at[0], halo_send.at[0])
    landed(kg.at[1], halo_send.at[1])
    landed(extra, extra_send)
    landed(recv1, send1)
    landed(part2.at[:3], send2)

    @pl.when(source_core != core)
    def _():
        landed(part2.at[3], send2)

    landed(recv3, send3)


def per_device(query_act, key_act, value_act, grad_out, filter_taps):
    channels = filter_taps.shape[1]
    ny = channels // (2 * W)
    nz = lax.axis_size("dp")
    own, prev, back = transforms()
    big = (1, T, channels)
    any_spec = pl.BlockSpec(memory_space=pl.ANY)
    vmem = pl.BlockSpec(memory_space=pltpu.VMEM)
    dma = pltpu.SemaphoreType.DMA
    outs = pl.pallas_call(
        functools.partial(kernel, nz, ny),
        out_shape=[jax.ShapeDtypeStruct(big, bf16)] * 4 + [jax.ShapeDtypeStruct((32, T), f32)],
        in_specs=[any_spec] * 8,
        out_specs=[vmem] * 5,
        scratch_shapes=[
            *[pltpu.VMEM((T, channels), bf16)] * 5,
            pltpu.VMEM((2 * F, 2 * T), bf16),
            pltpu.VMEM((2 * F, 2 * T), bf16),
            pltpu.VMEM((T, 6 * F), bf16),
            pltpu.VMEM((2 * F, 2 * T), bf16),
            pltpu.VMEM((2 * F, 2 * T), bf16),
            pltpu.VMEM((2, 2, ny, T, W), bf16),
            pltpu.VMEM((2, 2, ny, T, W), bf16),
            pltpu.VMEM((ny, T, W), bf16),
            *[pltpu.VMEM((2, ny, 2 * F, W), f32)] * 3,
            pltpu.VMEM((ny, T, W), bf16),
            pltpu.VMEM((ny - 1, T, W), bf16),
            pltpu.VMEM((4, 32, T), bf16),
            pltpu.VMEM((NX, 32, T), bf16),
            pltpu.VMEM((32, T), f32),
            pltpu.VMEM((nz - 1, 32, T), f32),
            dma((8,)), dma((2,)), dma((2, ny)), dma((2,)), dma(()), dma((ny,)),
            dma(()), dma(()), dma(()), dma((NX,)), dma(()), dma(()),
        ],
        compiler_params=pltpu.CompilerParams(
            collective_id=1, has_side_effects=True, vmem_limit_bytes=60 * 2**20
        ),
    )(query_act, key_act, value_act, grad_out, filter_taps, own, prev, back)
    return (*outs[:4], outs[4].T)


def solution(mesh):
    spread = P("dp", "ctx", None)
    return jax.shard_map(
        per_device, mesh=mesh, in_specs=(spread,) * 4 + (P(),),
        out_specs=(spread,) * 4 + (P(None, "ctx"),), check_vma=False,
    )
```

```python
import functools
import math

import jax
import jax.numpy as jnp
import ml_dtypes
import numpy as np
from jax import lax
from jax.experimental import pallas as pl
from jax.experimental.pallas import tpu as pltpu
from jax.sharding import PartitionSpec as P

MESH = pl.DeviceIdType.MESH
bf16 = jnp.bfloat16
f32 = jnp.float32
T = 128
F = 128
W = 256
NX = 4
VMEM_BYTES = 62 * 2**20
PIECES = 2


def split(matrix):
    hi = matrix.astype(ml_dtypes.bfloat16)
    lo = (matrix - hi.astype(np.float64)).astype(ml_dtypes.bfloat16)
    return hi, lo


def transforms():
    theta = np.pi * (2 * np.arange(F) + 1) / 256.0
    n = np.arange(T)

    def forward(shift):
        angle = theta[:, None] * (n + shift)[None, :]
        return np.concatenate([np.cos(angle), -np.sin(angle)], axis=0)

    own_hi, own_lo = split(forward(0))
    prev_hi, prev_lo = split(forward(-T))
    back_hi, back_lo = split(forward(0).T / F)
    return (
        np.concatenate([own_hi, own_lo], axis=1),
        np.concatenate([prev_hi, prev_lo], axis=1),
        np.concatenate([back_hi, back_hi, back_lo], axis=1),
    )


def kernel(
    nz, ny,
    q_hbm, k_hbm, v_hbm, g_hbm, h_hbm, own_hbm, prev_hbm, back_hbm,
    y_hbm, gq_hbm, gk_hbm, gv_hbm, gf_ref,
    q_ref, k_ref, v_ref, g_ref, h_ref, own_ref, prev_ref, back_ref,
    prev_kg, kg, halo, extra, spec, spec_h, early_sum, mates,
    part_x, recv_x, part_y, recv_y, part_z, recv_z,
    load_sem, const_sem, out_sem, halo_send, halo_recv, late_recv, extra_send, extra_recv,
    send_x, sem_x, send_y, sem_y, send_z, sem_z,
):
    z = lax.axis_index("dp")
    c = lax.axis_index("ctx")
    nc = ny * 2 * NX
    yy = c // (2 * NX)
    x = (c // 2) % NX
    core = c % 2
    near = 1 - core
    nb = ny // 2
    half = nb * W
    right = {"dp": z, "ctx": lax.rem(c + 1, nc)}
    left = {"dp": z, "ctx": lax.rem(c + nc - 1, nc)}
    partner = {"dp": z, "ctx": c + 1 - 2 * core}

    def at(y_to, x_to, core_to):
        return {"dp": z, "ctx": y_to * (2 * NX) + x_to * 2 + core_to}

    def at_x(d):
        return at(yy, lax.rem(x + d, NX), core)

    def at_z(d):
        return {"dp": lax.rem(z + d, nz), "ctx": c}

    def load(s):
        cols = pl.ds(pl.multiple_of(s * half, half), half)
        return [
            pltpu.make_async_copy(src.at[0, :, cols], dst.at[s], load_sem.at[s, i])
            for i, (src, dst) in enumerate(
                [(k_hbm, k_ref), (v_hbm, v_ref), (g_hbm, g_ref), (q_hbm, q_ref)]
            )
        ]

    for copy in load(near):
        copy.start()
    constants = [
        pltpu.make_async_copy(src, dst, const_sem.at[i])
        for i, (src, dst) in enumerate(
            [(own_hbm, own_ref), (h_hbm, h_ref), (prev_hbm, prev_ref), (back_hbm, back_ref)]
        )
    ]
    barrier = pltpu.get_barrier_semaphore()

    def greet(device):
        pl.semaphore_signal(barrier, inc=1, device_id=device, device_id_type=MESH)

    greet(left)
    greet(right)
    for d in range(1, NX):
        greet(at_x(d))
    for d in range(1, nz):
        greet(at_z(d))
    source_core = yy // nb
    own_source = source_core == core
    for ys in range(ny):
        @pl.when(jnp.logical_not(jnp.logical_and(ys == yy, own_source)))
        def _():
            greet(at(ys, x, source_core))

    def products(s):
        for j in range(nb):
            cols = slice(j * W, (j + 1) * W)
            b = s * nb + j
            kg[0, b] = (k_ref[s, :, cols].astype(f32) * v_ref[s, :, cols].astype(f32)).astype(bf16)
            kg[1, b] = (g_ref[s, :, cols].astype(f32) * q_ref[s, :, cols].astype(f32)).astype(bf16)

    for copy in load(near):
        copy.wait()
    for copy in load(core):
        copy.start()
    for copy in constants:
        copy.start()
    products(near)
    pl.semaphore_wait(barrier, 2 + (NX - 1) + (nz - 1) + jnp.where(own_source, ny - 1, ny))

    def halo_copy(array, b, device):
        return pltpu.make_async_remote_copy(
            src_ref=kg.at[array, b], dst_ref=halo.at[array, b],
            send_sem=halo_send.at[array], recv_sem=halo_recv.at[array, b % nb],
            device_id=device, device_id_type=MESH,
        )

    def late_copy(array, s, device):
        return pltpu.make_async_remote_copy(
            src_ref=kg.at[array, pl.ds(s * nb, nb)], dst_ref=halo.at[array, pl.ds(s * nb, nb)],
            send_sem=halo_send.at[array], recv_sem=late_recv.at[array],
            device_id=device, device_id_type=MESH,
        )

    def extra_copy(j):
        return pltpu.make_async_remote_copy(
            src_ref=kg.at[near, near * nb + j], dst_ref=extra.at[j],
            send_sem=extra_send, recv_sem=extra_recv.at[j],
            device_id=partner, device_id_type=MESH,
        )

    for j in range(nb):
        halo_copy(0, near * nb + j, right).start()
        halo_copy(1, near * nb + j, left).start()
        extra_copy(j).start()

    for copy in load(core):
        copy.wait()
    products(core)

    for copy in constants:
        copy.wait()
    prev_kg[0] = prev_ref[...] * jnp.where(c > 0, 1.0, 0.0).astype(bf16)
    prev_kg[1] = prev_ref[...] * jnp.where(c < nc - 1, -1.0, 0.0).astype(bf16)

    def forward(matrix, value):
        return jnp.dot(
            matrix, jnp.concatenate([value, value], axis=0), preferred_element_type=f32
        )

    def own_spectra(s):
        def step(j, carry):
            b = s * nb + j
            spec[0, b] = forward(own_ref[...], kg[0, b])
            spec[1, b] = forward(own_ref[...], kg[1, b])
            taps = h_ref[:, pl.ds(pl.multiple_of(b * W, W), W)]
            spec_h[b] = forward(own_ref[...], taps)
            return carry

        lax.fori_loop(0, nb, step, 0)

    own_spectra(core)
    own_spectra(near)

    def times(a, b):
        ar, ai, br, bi = a[:F], a[F:], b[:F], b[F:]
        return ar * br - ai * bi, ar * bi + ai * br

    def times_conj(a, b):
        ar, ai, br, bi = a[:F], a[F:], b[:F], b[F:]
        return ar * br + ai * bi, ai * br - ar * bi

    def inverse(re, im):
        value = jnp.concatenate([re, im], axis=0)
        hi = value.astype(bf16)
        lo = (value - hi.astype(f32)).astype(bf16)
        return jnp.dot(
            back_ref[...], jnp.concatenate([hi, lo, hi], axis=0), preferred_element_type=f32
        )

    first = core == 0

    def early_terms(j, carry):
        b = core * nb + j
        halo_copy(1 - core, b, partner).wait_recv()
        extra_copy(j).wait_recv()
        fast = forward(prev_kg[near], halo[near, b])
        other = forward(prev_ref[...], extra[j])
        own_k = spec[0, b]
        own_g = spec[1, b]
        spec[near, b] = spec[near, b] + fast
        re0, im0 = times_conj(jnp.where(first, own_g + fast, own_g), jnp.where(first, own_k, own_k + fast))
        re1, im1 = times_conj(jnp.where(first, -fast, other), jnp.where(first, other, fast))
        mates[j] = jnp.where(first, own_g, own_k)
        early_sum[j, :F] = re0 + re1
        early_sum[j, F:] = im0 + im1
        return carry

    lax.fori_loop(0, nb, early_terms, 0)

    def gradient(j, carry):
        b = core * nb + j
        halo_copy(core, b, partner).wait_recv()
        slow = forward(prev_kg[core], halo[core, b])
        own = spec[core, b]
        spec[core, b] = own + slow
        mate = mates[j]
        re, im = times_conj(jnp.where(first, mate, slow), jnp.where(first, slow, mate))
        value = inverse(early_sum[j, :F] + re, early_sum[j, F:] + im)
        part_x[j] = jnp.transpose(value).astype(bf16).reshape(NX, W // NX, T)
        for d in range(1, NX):
            pltpu.make_async_remote_copy(
                src_ref=part_x.at[j, lax.rem(x + d, NX)], dst_ref=recv_x.at[d - 1, j],
                send_sem=send_x, recv_sem=sem_x, device_id=at_x(d), device_id_type=MESH,
            ).start()
        return carry

    lax.fori_loop(0, nb, gradient, 0)
    late_copy(0, core, right).start()
    late_copy(1, core, left).start()

    def outputs(s):
        def step(j, carry):
            b = s * nb + j
            k_all = spec[0, b]
            g_all = spec[1, b]
            if s is near:
                k_all += forward(prev_kg[0], halo[0, b])
                g_all += forward(prev_kg[1], halo[1, b])
            taps = spec_h[b]
            cols = pl.ds(pl.multiple_of(j * W, W), W)
            m = inverse(*times(k_all, taps))
            q_ref[s, :, cols] = (q_ref[s, :, cols].astype(f32) * m).astype(bf16)
            g_ref[s, :, cols] = (g_ref[s, :, cols].astype(f32) * m).astype(bf16)
            m = inverse(*times_conj(g_all, taps))
            v_ref[s, :, cols] = (v_ref[s, :, cols].astype(f32) * m).astype(bf16)
            k_ref[s, :, cols] = (k_ref[s, :, cols].astype(f32) * m).astype(bf16)
            return carry

        lax.fori_loop(0, nb, step, 0)

    def store(s):
        cols = pl.ds(pl.multiple_of(s * half, half), half)
        return [
            pltpu.make_async_copy(src.at[s], dst.at[0, :, cols], out_sem.at[s, i])
            for i, (src, dst) in enumerate(
                [(q_ref, y_hbm), (g_ref, gq_hbm), (v_ref, gk_hbm), (k_ref, gv_hbm)]
            )
        ]

    def landed(ref, sem):
        pltpu.make_async_copy(ref, ref, sem).wait()

    outputs(core)
    for copy in store(core):
        copy.start()

    landed(recv_x, sem_x)
    for j in range(nb):
        total = part_x[j, x].astype(f32)
        for d in range(NX - 1):
            total += recv_x[d, j].astype(f32)
        part_y[j] = total.astype(bf16).reshape(2, W // NX // 2, T)
        for core_to in range(2):
            mine = jnp.logical_and(jnp.logical_and(own_source, yy == core * nb + j), core == core_to)

            @pl.when(jnp.logical_not(mine))
            def _():
                pltpu.make_async_remote_copy(
                    src_ref=part_y.at[j, core_to], dst_ref=recv_y.at[yy],
                    send_sem=send_y, recv_sem=sem_y.at[yy],
                    device_id=at(core * nb + j, x, core_to), device_id_type=MESH,
                ).start()

            @pl.when(mine)
            def _():
                recv_y[yy] = part_y[j, core_to]

    for ys in range(ny):
        @pl.when(jnp.logical_not(jnp.logical_and(ys == yy, own_source)))
        def _():
            landed(recv_y.at[ys], sem_y.at[ys])
    total = recv_y[0].astype(f32)
    for ys in range(1, ny):
        total += recv_y[ys].astype(f32)
    part_z[...] = total.astype(bf16)
    for d in range(1, nz):
        pltpu.make_async_remote_copy(
            src_ref=part_z, dst_ref=recv_z.at[d - 1], send_sem=send_z, recv_sem=sem_z,
            device_id=at_z(d), device_id_type=MESH,
        ).start()

    late_copy(0, near, right).wait_recv()
    late_copy(1, near, left).wait_recv()
    outputs(near)
    for copy in store(near):
        copy.start()

    landed(recv_z, sem_z)
    total = part_z[...].astype(f32)
    for d in range(nz - 1):
        total += recv_z[d].astype(f32)
    gf_ref[...] = total * (1.0 / math.sqrt(T * nc * nz))

    landed(kg.at[0], halo_send.at[0])
    landed(kg.at[1], halo_send.at[1])
    landed(extra, extra_send)
    landed(recv_x, send_x)
    landed(recv_y.at[pl.ds(0, ny - 1)], send_y)

    @pl.when(jnp.logical_not(own_source))
    def _():
        landed(recv_y.at[ny - 1], send_y)

    landed(recv_z, send_z)

    for s in (core, near):
        for copy in store(s):
            copy.wait()


def write_out(*refs):
    sources, targets, held, (load_sem, store_sem) = refs[:5], refs[5:10], refs[10:15], refs[15:]
    rows = T // PIECES
    loads, stores = [], []
    for i in range(5):
        for piece in range(PIECES if i < 4 else 1):
            at = (0, pl.ds(piece * rows, rows)) if i < 4 else ()
            loads.append(pltpu.make_async_copy(
                sources[i].at[at], held[i].at[at], load_sem.at[i, piece]))
            stores.append(pltpu.make_async_copy(
                held[i].at[at], targets[i].at[at], store_sem.at[i, piece]))
    for load in loads:
        load.start()
    for load, store in zip(loads, stores):
        load.wait()
        store.start()
    for store in stores:
        store.wait()


def per_device(query_act, key_act, value_act, grad_out, filter_taps):
    channels = filter_taps.shape[1]
    ny = channels // W
    nz = lax.axis_size("dp")
    own, prev, back = transforms()
    big = jax.ShapeDtypeStruct((1, T, channels), bf16)
    half = channels // 2
    cols = W // NX // 2
    small = jax.ShapeDtypeStruct((cols, T), f32)
    hbm = pl.BlockSpec(memory_space=pl.ANY)
    vmem = pl.BlockSpec(memory_space=pltpu.VMEM)
    dma = pltpu.SemaphoreType.DMA
    limit = VMEM_BYTES
    outs = pl.pallas_call(
        functools.partial(kernel, nz, ny),
        out_shape=[big] * 4 + [small],
        in_specs=[hbm] * 8,
        out_specs=[hbm] * 4 + [vmem],
        scratch_shapes=[
            *[pltpu.VMEM((2, T, half), bf16)] * 4,
            pltpu.VMEM((T, channels), bf16),
            pltpu.VMEM((2 * F, 2 * T), bf16),
            pltpu.VMEM((2 * F, 2 * T), bf16),
            pltpu.VMEM((T, 6 * F), bf16),
            pltpu.VMEM((2, 2 * F, 2 * T), bf16),
            pltpu.VMEM((2, ny, T, W), bf16),
            pltpu.VMEM((2, ny, T, W), bf16),
            pltpu.VMEM((ny // 2, T, W), bf16),
            pltpu.VMEM((2, ny, 2 * F, W), f32),
            pltpu.VMEM((ny, 2 * F, W), f32),
            pltpu.VMEM((ny // 2, 2 * F, W), f32),
            pltpu.VMEM((ny // 2, 2 * F, W), f32),
            pltpu.VMEM((ny // 2, NX, W // NX, T), bf16),
            pltpu.VMEM((NX - 1, ny // 2, W // NX, T), bf16),
            pltpu.VMEM((ny // 2, 2, cols, T), bf16),
            pltpu.VMEM((ny, cols, T), bf16),
            pltpu.VMEM((cols, T), bf16),
            pltpu.VMEM((nz - 1, cols, T), bf16),
            dma((2, 4)), dma((4,)), dma((2, 4)), dma((2,)), dma((2, ny // 2)), dma((2,)),
            dma(()), dma((ny // 2,)), dma(()), dma(()), dma(()), dma((ny,)), dma(()), dma(()),
        ],
        compiler_params=pltpu.CompilerParams(
            collective_id=1, has_side_effects=True, vmem_limit_bytes=limit
        ),
    )(query_act, key_act, value_act, grad_out, filter_taps, own, prev, back)
    *done, summed = pl.pallas_call(
        write_out,
        out_shape=[big] * 4 + [small],
        in_specs=[hbm] * 5,
        out_specs=[hbm] * 5,
        scratch_shapes=[pltpu.VMEM(big.shape, bf16)] * 4 + [pltpu.VMEM(small.shape, f32)] + [dma((5, PIECES))] * 2,
        compiler_params=pltpu.CompilerParams(vmem_limit_bytes=limit),
    )(*outs)
    return (*done, summed.T)


def solution(mesh):
    spread = P("dp", "ctx", None)
    return jax.shard_map(
        per_device, mesh=mesh, in_specs=(spread,) * 4 + (P(),),
        out_specs=(spread,) * 4 + (P(None, "ctx"),), check_vma=False,
    )
```

```python
import functools
import math

import jax
import jax.numpy as jnp
import ml_dtypes
import numpy as np
from jax import lax
from jax.experimental import pallas as pl
from jax.experimental.pallas import tpu as pltpu
from jax.sharding import PartitionSpec as P

MESH = pl.DeviceIdType.MESH
bf16 = jnp.bfloat16
f32 = jnp.float32
T = 128
F = 128
W = 256
NX = 4
VMEM_BYTES = 64929792
PIECES = 2
PIECES = 2
PIECES = 2
PIECES = 2


def split(matrix):
    hi = matrix.astype(ml_dtypes.bfloat16)
    lo = (matrix - hi.astype(np.float64)).astype(ml_dtypes.bfloat16)
    return hi, lo


def transforms():
    theta = np.pi * (2 * np.arange(F) + 1) / 256.0
    n = np.arange(T)

    def forward(shift):
        angle = theta[:, None] * (n + shift)[None, :]
        return np.concatenate([np.cos(angle), -np.sin(angle)], axis=0)

    own_hi, own_lo = split(forward(0))
    prev_hi, prev_lo = split(forward(-T))
    back_hi, back_lo = split(forward(0).T / F)
    return (
        np.concatenate([own_hi, own_lo], axis=1),
        np.concatenate([prev_hi, prev_lo], axis=1),
        np.concatenate([back_hi, back_hi, back_lo], axis=1),
    )


def kernel(
    nz, ny,
    q_hbm, k_hbm, v_hbm, g_hbm, h_hbm, own_hbm, prev_hbm, back_hbm,
    y_hbm, gq_hbm, gk_hbm, gv_hbm, gf_ref,
    q_ref, k_ref, v_ref, g_ref, h_ref, own_ref, prev_ref, back_ref,
    prev_kg, kg, halo, extra, spec, spec_h, early_sum, mates,
    part_x, recv_x, part_y, recv_y, part_z, recv_z,
    load_sem, const_sem, halo_send, halo_recv, late_recv, extra_send, extra_recv,
    send_x, sem_x, send_y, sem_y, send_z, sem_z,
):
    z = lax.axis_index("dp")
    c = lax.axis_index("ctx")
    nc = ny * 2 * NX
    yy = c // (2 * NX)
    x = (c // 2) % NX
    core = c % 2
    near = 1 - core
    nb = ny // 2
    half = nb * W
    right = {"dp": z, "ctx": lax.rem(c + 1, nc)}
    left = {"dp": z, "ctx": lax.rem(c + nc - 1, nc)}
    partner = {"dp": z, "ctx": c + 1 - 2 * core}
    far = {"dp": z, "ctx": lax.rem(c + 2 * core - 1 + nc, nc)}

    def at(y_to, x_to, core_to):
        return {"dp": z, "ctx": y_to * (2 * NX) + x_to * 2 + core_to}

    def at_x(d):
        return at(yy, lax.rem(x + d, NX), core)

    def at_z(d):
        return {"dp": lax.rem(z + d, nz), "ctx": c}

    def load(s):
        cols = pl.ds(pl.multiple_of(s * half, half), half)
        return [
            pltpu.make_async_copy(src.at[0, :, cols], dst.at[s], load_sem.at[s, i])
            for i, (src, dst) in enumerate(
                [(k_hbm, k_ref), (v_hbm, v_ref), (g_hbm, g_ref), (q_hbm, q_ref)]
            )
        ]

    for copy in load(near):
        copy.start()
    constants = [
        pltpu.make_async_copy(src, dst, const_sem.at[i])
        for i, (src, dst) in enumerate(
            [(own_hbm, own_ref), (h_hbm, h_ref), (prev_hbm, prev_ref), (back_hbm, back_ref)]
        )
    ]
    barrier = pltpu.get_barrier_semaphore()

    def greet(device):
        pl.semaphore_signal(barrier, inc=1, device_id=device, device_id_type=MESH)

    greet(left)
    greet(right)
    for d in range(1, NX):
        greet(at_x(d))
    for d in range(1, nz):
        greet(at_z(d))
    source_core = yy // nb
    own_source = source_core == core
    for ys in range(ny):
        @pl.when(jnp.logical_not(jnp.logical_and(ys == yy, own_source)))
        def _():
            greet(at(ys, x, source_core))

    def products(s):
        for j in range(nb):
            cols = slice(j * W, (j + 1) * W)
            b = s * nb + j
            kg[0, b] = (k_ref[s, :, cols].astype(f32) * v_ref[s, :, cols].astype(f32)).astype(bf16)
            kg[1, b] = (g_ref[s, :, cols].astype(f32) * q_ref[s, :, cols].astype(f32)).astype(bf16)

    for copy in load(near):
        copy.wait()
    for copy in load(core):
        copy.start()
    for copy in constants:
        copy.start()
    products(near)
    pl.semaphore_wait(barrier, 2 + (NX - 1) + (nz - 1) + jnp.where(own_source, ny - 1, ny))

    def halo_copy(array, b, device):
        return pltpu.make_async_remote_copy(
            src_ref=kg.at[array, b], dst_ref=halo.at[array, b],
            send_sem=halo_send.at[array], recv_sem=halo_recv.at[array, b % nb],
            device_id=device, device_id_type=MESH,
        )

    def late_copy(array, s, device):
        return pltpu.make_async_remote_copy(
            src_ref=kg.at[array, pl.ds(s * nb, nb)], dst_ref=halo.at[array, pl.ds(s * nb, nb)],
            send_sem=halo_send.at[array], recv_sem=late_recv.at[array],
            device_id=device, device_id_type=MESH,
        )

    def extra_copy(j):
        return pltpu.make_async_remote_copy(
            src_ref=kg.at[near, near * nb + j], dst_ref=extra.at[j],
            send_sem=extra_send, recv_sem=extra_recv.at[j],
            device_id=partner, device_id_type=MESH,
        )

    for j in range(nb):
        halo_copy(near, near * nb + j, far).start()
    for j in range(nb):
        halo_copy(core, near * nb + j, partner).start()
        extra_copy(j).start()

    for copy in load(core):
        copy.wait()
    products(core)

    for copy in constants:
        copy.wait()
    prev_kg[0] = prev_ref[...] * jnp.where(c > 0, 1.0, 0.0).astype(bf16)
    prev_kg[1] = prev_ref[...] * jnp.where(c < nc - 1, -1.0, 0.0).astype(bf16)

    def forward(matrix, value):
        return jnp.dot(
            matrix, jnp.concatenate([value, value], axis=0), preferred_element_type=f32
        )

    def own_spectra(s):
        def step(j, carry):
            b = s * nb + j
            spec[0, b] = forward(own_ref[...], kg[0, b])
            spec[1, b] = forward(own_ref[...], kg[1, b])
            return carry

        lax.fori_loop(0, nb, step, 0)

    def tap_spectra(s):
        def step(j, carry):
            b = s * nb + j
            taps = h_ref[:, pl.ds(pl.multiple_of(b * W, W), W)]
            spec_h[b] = forward(own_ref[...], taps)
            return carry

        lax.fori_loop(0, nb, step, 0)

    own_spectra(core)

    def times(a, b):
        ar, ai, br, bi = a[:F], a[F:], b[:F], b[F:]
        return ar * br - ai * bi, ar * bi + ai * br

    def times_conj(a, b):
        ar, ai, br, bi = a[:F], a[F:], b[:F], b[F:]
        return ar * br + ai * bi, ai * br - ar * bi

    def inverse(re, im):
        value = jnp.concatenate([re, im], axis=0)
        hi = value.astype(bf16)
        lo = (value - hi.astype(f32)).astype(bf16)
        return jnp.dot(
            back_ref[...], jnp.concatenate([hi, lo, hi], axis=0), preferred_element_type=f32
        )

    first = core == 0

    def early_terms(j, carry):
        b = core * nb + j
        halo_copy(1 - core, b, partner).wait_recv()
        extra_copy(j).wait_recv()
        fast = forward(prev_kg[near], halo[near, b])
        other = forward(prev_ref[...], extra[j])
        own_k = spec[0, b]
        own_g = spec[1, b]
        spec[near, b] = spec[near, b] + fast
        re0, im0 = times_conj(jnp.where(first, own_g + fast, own_g), jnp.where(first, own_k, own_k + fast))
        re1, im1 = times_conj(jnp.where(first, -fast, other), jnp.where(first, other, fast))
        mates[j] = jnp.where(first, own_g, own_k)
        early_sum[j, :F] = re0 + re1
        early_sum[j, F:] = im0 + im1
        return carry

    lax.fori_loop(0, nb, early_terms, 0)

    def gradient(j, carry):
        b = core * nb + j
        halo_copy(core, b, partner).wait_recv()
        slow = forward(prev_kg[core], halo[core, b])
        own = spec[core, b]
        spec[core, b] = own + slow
        mate = mates[j]
        re, im = times_conj(jnp.where(first, mate, slow), jnp.where(first, slow, mate))
        value = inverse(early_sum[j, :F] + re, early_sum[j, F:] + im)
        part_x[j] = jnp.transpose(value).astype(bf16).reshape(NX, W // NX, T)
        for d in (2, 1, 3):
            pltpu.make_async_remote_copy(
                src_ref=part_x.at[j, lax.rem(x + d, NX)], dst_ref=recv_x.at[d - 1, j],
                send_sem=send_x, recv_sem=sem_x, device_id=at_x(d), device_id_type=MESH,
            ).start()
        return carry

    lax.fori_loop(0, nb, gradient, 0)

    def outputs(s):
        def step(j, carry):
            b = s * nb + j
            k_all = spec[0, b]
            g_all = spec[1, b]
            if s is near:
                k_all += forward(prev_kg[0], halo[0, b])
                g_all += forward(prev_kg[1], halo[1, b])
            taps = spec_h[b]
            cols = pl.ds(pl.multiple_of(j * W, W), W)
            full = pl.ds(pl.multiple_of(b * W, W), W)
            m = inverse(*times(k_all, taps))
            y_hbm[0, :, full] = (q_ref[s, :, cols].astype(f32) * m).astype(bf16)
            gq_hbm[0, :, full] = (g_ref[s, :, cols].astype(f32) * m).astype(bf16)
            m = inverse(*times_conj(g_all, taps))
            gk_hbm[0, :, full] = (v_ref[s, :, cols].astype(f32) * m).astype(bf16)
            gv_hbm[0, :, full] = (k_ref[s, :, cols].astype(f32) * m).astype(bf16)
            return carry

        lax.fori_loop(0, nb, step, 0)

    def landed(ref, sem):
        pltpu.make_async_copy(ref, ref, sem).wait()

    tap_spectra(core)
    outputs(core)

    landed(recv_x, sem_x)
    for i in range(nb):
        j = lax.rem(yy + i + jnp.where(own_source, 1, 0), nb)
        total = part_x[j, x].astype(f32)
        for d in range(NX - 1):
            total += recv_x[d, j].astype(f32)
        part_y[j] = total.astype(bf16).reshape(2, W // NX // 2, T)
        for core_to in range(2):
            mine = jnp.logical_and(jnp.logical_and(own_source, yy == core * nb + j), core == core_to)

            @pl.when(jnp.logical_not(mine))
            def _():
                pltpu.make_async_remote_copy(
                    src_ref=part_y.at[j, core_to], dst_ref=recv_y.at[yy],
                    send_sem=send_y, recv_sem=sem_y.at[yy],
                    device_id=at(core * nb + j, x, core_to), device_id_type=MESH,
                ).start()

            @pl.when(mine)
            def _():
                recv_y[yy] = part_y[j, core_to]

    late_copy(0, core, right).start()
    late_copy(1, core, left).start()
    own_spectra(near)
    tap_spectra(near)

    for ys in range(ny):
        @pl.when(jnp.logical_not(jnp.logical_and(ys == yy, own_source)))
        def _():
            landed(recv_y.at[ys], sem_y.at[ys])
    total = recv_y[0].astype(f32)
    for ys in range(1, ny):
        total += recv_y[ys].astype(f32)
    part_z[...] = total.astype(bf16)
    for d in sorted(range(1, nz), key=lambda d: abs(d - nz // 2)):
        pltpu.make_async_remote_copy(
            src_ref=part_z, dst_ref=recv_z.at[d - 1], send_sem=send_z, recv_sem=sem_z,
            device_id=at_z(d), device_id_type=MESH,
        ).start()

    late_copy(0, near, right).wait_recv()
    late_copy(1, near, left).wait_recv()
    outputs(near)

    landed(recv_z, sem_z)
    total = part_z[...].astype(f32)
    for d in range(nz - 1):
        total += recv_z[d].astype(f32)
    gf_ref[...] = total * (1.0 / math.sqrt(T * nc * nz))

    landed(kg.at[0], halo_send.at[0])
    landed(kg.at[1], halo_send.at[1])
    landed(extra, extra_send)
    landed(recv_x, send_x)
    landed(recv_y.at[pl.ds(0, ny - 1)], send_y)

    @pl.when(jnp.logical_not(own_source))
    def _():
        landed(recv_y.at[ny - 1], send_y)

    landed(recv_z, send_z)


def write_out(*refs):
    sem = refs[10]
    copies = [pltpu.make_async_copy(refs[i], refs[5 + i], sem.at[i]) for i in range(5)]
    for copy in copies:
        copy.start()
    for copy in copies:
        copy.wait()


def per_device(query_act, key_act, value_act, grad_out, filter_taps):
    channels = filter_taps.shape[1]
    ny = channels // W
    nz = lax.axis_size("dp")
    own, prev, back = transforms()
    big = jax.ShapeDtypeStruct((1, T, channels), bf16)
    half = channels // 2
    cols = W // NX // 2
    small = jax.ShapeDtypeStruct((cols, T), f32)
    hbm = pl.BlockSpec(memory_space=pl.ANY)
    vmem = pl.BlockSpec(memory_space=pltpu.VMEM)
    dma = pltpu.SemaphoreType.DMA
    limit = VMEM_BYTES
    outs = pl.pallas_call(
        functools.partial(kernel, nz, ny),
        out_shape=[pltpu.VMEM(big.shape, bf16)] * 4 + [pltpu.VMEM(small.shape, f32)],
        in_specs=[hbm] * 8,
        out_specs=[vmem] * 5,
        scratch_shapes=[
            *[pltpu.VMEM((2, T, half), bf16)] * 4,
            pltpu.VMEM((T, channels), bf16),
            pltpu.VMEM((2 * F, 2 * T), bf16),
            pltpu.VMEM((2 * F, 2 * T), bf16),
            pltpu.VMEM((T, 6 * F), bf16),
            pltpu.VMEM((2, 2 * F, 2 * T), bf16),
            pltpu.VMEM((2, ny, T, W), bf16),
            pltpu.VMEM((2, ny, T, W), bf16),
            pltpu.VMEM((ny // 2, T, W), bf16),
            pltpu.VMEM((2, ny, 2 * F, W), f32),
            pltpu.VMEM((ny, 2 * F, W), f32),
            pltpu.VMEM((ny // 2, 2 * F, W), f32),
            pltpu.VMEM((ny // 2, 2 * F, W), f32),
            pltpu.VMEM((ny // 2, NX, W // NX, T), bf16),
            pltpu.VMEM((NX - 1, ny // 2, W // NX, T), bf16),
            pltpu.VMEM((ny // 2, 2, cols, T), bf16),
            pltpu.VMEM((ny, cols, T), bf16),
            pltpu.VMEM((cols, T), bf16),
            pltpu.VMEM((nz - 1, cols, T), bf16),
            dma((2, 4)), dma((4,)), dma((2,)), dma((2, ny // 2)), dma((2,)),
            dma(()), dma((ny // 2,)), dma(()), dma(()), dma(()), dma((ny,)), dma(()), dma(()),
        ],
        compiler_params=pltpu.CompilerParams(
            collective_id=1, has_side_effects=True, vmem_limit_bytes=limit
        ),
    )(query_act, key_act, value_act, grad_out, filter_taps, own, prev, back)
    *done, summed = pl.pallas_call(
        write_out,
        out_shape=[big] * 4 + [small],
        in_specs=[vmem] * 5,
        out_specs=[hbm] * 5,
        scratch_shapes=[dma((5,))],
        compiler_params=pltpu.CompilerParams(vmem_limit_bytes=2**20),
    )(*outs)
    return (*done, summed.T)


def solution(mesh):
    spread = P("dp", "ctx", None)
    return jax.shard_map(
        per_device, mesh=mesh, in_specs=(spread,) * 4 + (P(),),
        out_specs=(spread,) * 4 + (P(None, "ctx"),), check_vma=False,
    )
```

```python
import functools
import math

import jax
import jax.numpy as jnp
import ml_dtypes
import numpy as np
from jax import lax
from jax.experimental import pallas as pl
from jax.experimental.pallas import tpu as pltpu
from jax.sharding import PartitionSpec as P

MESH = pl.DeviceIdType.MESH
bf16 = jnp.bfloat16
f32 = jnp.float32
T = 128
F = 128
W = 256
NX = 4
VMEM_BYTES = 64929792
PIECES = 2
PIECES = 2
PIECES = 2
PIECES = 2


def split(matrix):
    hi = matrix.astype(ml_dtypes.bfloat16)
    lo = (matrix - hi.astype(np.float64)).astype(ml_dtypes.bfloat16)
    return hi, lo


def transforms():
    theta = np.pi * (2 * np.arange(F) + 1) / 256.0
    n = np.arange(T)

    def forward(shift):
        angle = theta[:, None] * (n + shift)[None, :]
        return np.concatenate([np.cos(angle), -np.sin(angle)], axis=0)

    own_hi, own_lo = split(forward(0))
    prev_hi, prev_lo = split(forward(-T))
    back_hi, back_lo = split(forward(0).T / F)
    return (
        np.concatenate([own_hi, own_lo], axis=1),
        np.concatenate([prev_hi, prev_lo], axis=1),
        np.concatenate([back_hi, back_hi, back_lo], axis=1),
    )


def kernel(
    nz, ny,
    q_hbm, k_hbm, v_hbm, g_hbm, h_hbm, own_hbm, prev_hbm, back_hbm,
    y_hbm, gq_hbm, gk_hbm, gv_hbm, gf_ref,
    q_ref, k_ref, v_ref, g_ref, h_ref, own_ref, prev_ref, back_ref,
    prev_kg, kg, halo, extra, spec, spec_h, early_sum, mates,
    part_x, recv_x, part_y, recv_y, part_z, recv_z,
    load_sem, const_sem, halo_send, halo_recv, late_recv, extra_send, extra_recv,
    send_x, sem_x, send_y, sem_y, send_z, sem_z,
):
    z = lax.axis_index("dp")
    c = lax.axis_index("ctx")
    nc = ny * 2 * NX
    yy = c // (2 * NX)
    x = (c // 2) % NX
    core = c % 2
    near = 1 - core
    nb = ny // 2
    half = nb * W
    right = {"dp": z, "ctx": lax.rem(c + 1, nc)}
    left = {"dp": z, "ctx": lax.rem(c + nc - 1, nc)}
    partner = {"dp": z, "ctx": c + 1 - 2 * core}
    far = {"dp": z, "ctx": lax.rem(c + 2 * core - 1 + nc, nc)}

    def at(y_to, x_to, core_to):
        return {"dp": z, "ctx": y_to * (2 * NX) + x_to * 2 + core_to}

    def at_x(d):
        return at(yy, lax.rem(x + d, NX), core)

    def at_z(d):
        return {"dp": lax.rem(z + d, nz), "ctx": c}

    def load(s):
        cols = pl.ds(pl.multiple_of(s * half, half), half)
        return [
            pltpu.make_async_copy(src.at[0, :, cols], dst.at[s], load_sem.at[s, i])
            for i, (src, dst) in enumerate(
                [(k_hbm, k_ref), (v_hbm, v_ref), (g_hbm, g_ref), (q_hbm, q_ref)]
            )
        ]

    for copy in load(near):
        copy.start()
    constants = [
        pltpu.make_async_copy(src, dst, const_sem.at[i])
        for i, (src, dst) in enumerate(
            [(own_hbm, own_ref), (h_hbm, h_ref), (prev_hbm, prev_ref), (back_hbm, back_ref)]
        )
    ]
    barrier = pltpu.get_barrier_semaphore()

    def greet(device):
        pl.semaphore_signal(barrier, inc=1, device_id=device, device_id_type=MESH)

    source_core = yy // nb
    own_source = source_core == core
    greet(left)
    greet(right)
    for d in sorted(range(ny), key=lambda d: abs(d - ny // 2)):
        ys = lax.rem(yy + d, ny)
        if d:
            greet(at(ys, x, source_core))
        else:
            @pl.when(jnp.logical_not(own_source))
            def _():
                greet(at(ys, x, source_core))
    for d in (2, 1, 3):
        greet(at_x(d))
    for d in sorted(range(1, nz), key=lambda d: abs(d - nz // 2)):
        greet(at_z(d))

    def products(s):
        for j in range(nb):
            cols = slice(j * W, (j + 1) * W)
            b = s * nb + j
            kg[0, b] = (k_ref[s, :, cols].astype(f32) * v_ref[s, :, cols].astype(f32)).astype(bf16)
            kg[1, b] = (g_ref[s, :, cols].astype(f32) * q_ref[s, :, cols].astype(f32)).astype(bf16)

    for copy in load(near):
        copy.wait()
    for copy in load(core):
        copy.start()
    for copy in constants:
        copy.start()
    products(near)
    pl.semaphore_wait(barrier, 2 + (NX - 1) + (nz - 1) + jnp.where(own_source, ny - 1, ny))

    def halo_copy(array, b, device):
        return pltpu.make_async_remote_copy(
            src_ref=kg.at[array, b], dst_ref=halo.at[array, b],
            send_sem=halo_send.at[array], recv_sem=halo_recv.at[array, b % nb],
            device_id=device, device_id_type=MESH,
        )

    def late_copy(array, b, device):
        return pltpu.make_async_remote_copy(
            src_ref=kg.at[array, b], dst_ref=halo.at[array, b],
            send_sem=halo_send.at[array], recv_sem=late_recv.at[array, b % nb],
            device_id=device, device_id_type=MESH,
        )

    def send_late(first_block, last_block):
        for j in range(first_block, last_block):
            late_copy(near, core * nb + j, far).start()

    def send_near():
        for j in range(nb):
            late_copy(core, core * nb + j, partner).start()

    turn = x == jnp.where(core == 1, NX - 1, 0)

    def extra_copy(j):
        return pltpu.make_async_remote_copy(
            src_ref=kg.at[near, near * nb + j], dst_ref=extra.at[j],
            send_sem=extra_send, recv_sem=extra_recv.at[j],
            device_id=partner, device_id_type=MESH,
        )

    for j in range(nb):
        halo_copy(near, near * nb + j, far).start()
    for j in range(nb):
        halo_copy(core, near * nb + j, partner).start()
        extra_copy(j).start()

    for copy in load(core):
        copy.wait()
    products(core)

    for copy in constants:
        copy.wait()
    prev_kg[0] = prev_ref[...] * jnp.where(c > 0, 1.0, 0.0).astype(bf16)
    prev_kg[1] = prev_ref[...] * jnp.where(c < nc - 1, -1.0, 0.0).astype(bf16)

    def forward(matrix, value):
        return jnp.dot(
            matrix, jnp.concatenate([value, value], axis=0), preferred_element_type=f32
        )

    def own_spectra(s):
        def step(j, carry):
            b = s * nb + j
            spec[0, b] = forward(own_ref[...], kg[0, b])
            spec[1, b] = forward(own_ref[...], kg[1, b])
            return carry

        lax.fori_loop(0, nb, step, 0)

    def tap_spectra(s):
        def step(j, carry):
            b = s * nb + j
            taps = h_ref[:, pl.ds(pl.multiple_of(b * W, W), W)]
            spec_h[b] = forward(own_ref[...], taps)
            return carry

        lax.fori_loop(0, nb, step, 0)

    own_spectra(core)

    def times(a, b):
        ar, ai, br, bi = a[:F], a[F:], b[:F], b[F:]
        return ar * br - ai * bi, ar * bi + ai * br

    def times_conj(a, b):
        ar, ai, br, bi = a[:F], a[F:], b[:F], b[F:]
        return ar * br + ai * bi, ai * br - ar * bi

    def inverse(re, im):
        value = jnp.concatenate([re, im], axis=0)
        hi = value.astype(bf16)
        lo = (value - hi.astype(f32)).astype(bf16)
        return jnp.dot(
            back_ref[...], jnp.concatenate([hi, lo, hi], axis=0), preferred_element_type=f32
        )

    first = core == 0

    def early_terms(j, carry):
        b = core * nb + j
        halo_copy(1 - core, b, partner).wait_recv()
        extra_copy(j).wait_recv()
        fast = forward(prev_kg[near], halo[near, b])
        other = forward(prev_ref[...], extra[j])
        own_k = spec[0, b]
        own_g = spec[1, b]
        spec[near, b] = spec[near, b] + fast
        re0, im0 = times_conj(jnp.where(first, own_g + fast, own_g), jnp.where(first, own_k, own_k + fast))
        re1, im1 = times_conj(jnp.where(first, -fast, other), jnp.where(first, other, fast))
        mates[j] = jnp.where(first, own_g, own_k)
        early_sum[j, :F] = re0 + re1
        early_sum[j, F:] = im0 + im1
        return carry

    lax.fori_loop(0, nb, early_terms, 0)

    def gradient(j, carry):
        b = core * nb + j
        halo_copy(core, b, partner).wait_recv()
        slow = forward(prev_kg[core], halo[core, b])
        own = spec[core, b]
        spec[core, b] = own + slow
        mate = mates[j]
        re, im = times_conj(jnp.where(first, mate, slow), jnp.where(first, slow, mate))
        value = inverse(early_sum[j, :F] + re, early_sum[j, F:] + im)
        part_x[j] = jnp.transpose(value).astype(bf16).reshape(NX, W // NX, T)
        for d in (2, 1, 3):
            pltpu.make_async_remote_copy(
                src_ref=part_x.at[j, lax.rem(x + d, NX)], dst_ref=recv_x.at[j, d - 1],
                send_sem=send_x, recv_sem=sem_x.at[j], device_id=at_x(d), device_id_type=MESH,
            ).start()
        return carry

    lax.fori_loop(0, nb, gradient, 0)
    @pl.when(turn)
    def _():
        send_late(0, nb // 2)


    def outputs(s, first_block, last_block):
        def step(j, carry):
            b = s * nb + j
            if s is near:
                late_copy(0, b, right).wait_recv()
                late_copy(1, b, left).wait_recv()
            k_all = spec[0, b]
            g_all = spec[1, b]
            if s is near:
                k_all += forward(prev_kg[0], halo[0, b])
                g_all += forward(prev_kg[1], halo[1, b])
            taps = spec_h[b]
            cols = pl.ds(pl.multiple_of(j * W, W), W)
            full = pl.ds(pl.multiple_of(b * W, W), W)
            m = inverse(*times(k_all, taps))
            y_hbm[0, :, full] = (q_ref[s, :, cols].astype(f32) * m).astype(bf16)
            gq_hbm[0, :, full] = (g_ref[s, :, cols].astype(f32) * m).astype(bf16)
            m = inverse(*times_conj(g_all, taps))
            gk_hbm[0, :, full] = (v_ref[s, :, cols].astype(f32) * m).astype(bf16)
            gv_hbm[0, :, full] = (k_ref[s, :, cols].astype(f32) * m).astype(bf16)
            return carry

        lax.fori_loop(first_block, last_block, step, 0)

    def landed(ref, sem):
        pltpu.make_async_copy(ref, ref, sem).wait()

    own_spectra(near)

    for j in range(nb):
        landed(recv_x.at[j], sem_x.at[j])
        total = part_x[j, x].astype(f32)
        for d in range(NX - 1):
            total += recv_x[j, d].astype(f32)
        part_y[j] = total.astype(bf16).reshape(2, W // NX // 2, T)
        for core_to in range(2):
            mine = jnp.logical_and(jnp.logical_and(own_source, yy == core * nb + j), core == core_to)

            @pl.when(jnp.logical_not(mine))
            def _():
                pltpu.make_async_remote_copy(
                    src_ref=part_y.at[j, core_to], dst_ref=recv_y.at[yy],
                    send_sem=send_y, recv_sem=sem_y.at[yy],
                    device_id=at(core * nb + j, x, core_to), device_id_type=MESH,
                ).start()

            @pl.when(mine)
            def _():
                recv_y[yy] = part_y[j, core_to]

    send_near()
    @pl.when(jnp.logical_not(turn))
    def _():
        send_late(0, nb)

    tap_spectra(core)
    tap_spectra(near)
    outputs(core, 0, nb)

    for ys in range(ny):
        @pl.when(jnp.logical_not(jnp.logical_and(ys == yy, own_source)))
        def _():
            landed(recv_y.at[ys], sem_y.at[ys])
    total = recv_y[0].astype(f32)
    for ys in range(1, ny):
        total += recv_y[ys].astype(f32)
    part_z[...] = total.astype(bf16)
    for d in sorted(range(1, nz), key=lambda d: abs(d - nz // 2)):
        pltpu.make_async_remote_copy(
            src_ref=part_z, dst_ref=recv_z.at[d - 1], send_sem=send_z, recv_sem=sem_z,
            device_id=at_z(d), device_id_type=MESH,
        ).start()

    @pl.when(turn)
    def _():
        send_late(nb // 2, nb)

    outputs(near, 0, nb)

    landed(recv_z, sem_z)
    total = part_z[...].astype(f32)
    for d in range(nz - 1):
        total += recv_z[d].astype(f32)
    gf_ref[...] = total * (1.0 / math.sqrt(T * nc * nz))

    landed(kg.at[0], halo_send.at[0])
    landed(kg.at[1], halo_send.at[1])
    landed(extra, extra_send)
    landed(recv_x, send_x)
    landed(recv_y.at[pl.ds(0, ny - 1)], send_y)

    @pl.when(jnp.logical_not(own_source))
    def _():
        landed(recv_y.at[ny - 1], send_y)

    landed(recv_z, send_z)


def write_out(*refs):
    sem = refs[10]
    copies = [pltpu.make_async_copy(refs[i], refs[5 + i], sem.at[i]) for i in range(5)]
    for copy in copies:
        copy.start()
    for copy in copies:
        copy.wait()


def per_device(query_act, key_act, value_act, grad_out, filter_taps):
    channels = filter_taps.shape[1]
    ny = channels // W
    nz = lax.axis_size("dp")
    own, prev, back = transforms()
    big = jax.ShapeDtypeStruct((1, T, channels), bf16)
    half = channels // 2
    cols = W // NX // 2
    small = jax.ShapeDtypeStruct((cols, T), f32)
    hbm = pl.BlockSpec(memory_space=pl.ANY)
    vmem = pl.BlockSpec(memory_space=pltpu.VMEM)
    dma = pltpu.SemaphoreType.DMA
    limit = VMEM_BYTES
    outs = pl.pallas_call(
        functools.partial(kernel, nz, ny),
        out_shape=[pltpu.VMEM(big.shape, bf16)] * 4 + [pltpu.VMEM(small.shape, f32)],
        in_specs=[hbm] * 8,
        out_specs=[vmem] * 5,
        scratch_shapes=[
            *[pltpu.VMEM((2, T, half), bf16)] * 4,
            pltpu.VMEM((T, channels), bf16),
            pltpu.VMEM((2 * F, 2 * T), bf16),
            pltpu.VMEM((2 * F, 2 * T), bf16),
            pltpu.VMEM((T, 6 * F), bf16),
            pltpu.VMEM((2, 2 * F, 2 * T), bf16),
            pltpu.VMEM((2, ny, T, W), bf16),
            pltpu.VMEM((2, ny, T, W), bf16),
            pltpu.VMEM((ny // 2, T, W), bf16),
            pltpu.VMEM((2, ny, 2 * F, W), f32),
            pltpu.VMEM((ny, 2 * F, W), f32),
            pltpu.VMEM((ny // 2, 2 * F, W), f32),
            pltpu.VMEM((ny // 2, 2 * F, W), f32),
            pltpu.VMEM((ny // 2, NX, W // NX, T), bf16),
            pltpu.VMEM((ny // 2, NX - 1, W // NX, T), bf16),
            pltpu.VMEM((ny // 2, 2, cols, T), bf16),
            pltpu.VMEM((ny, cols, T), bf16),
            pltpu.VMEM((cols, T), bf16),
            pltpu.VMEM((nz - 1, cols, T), bf16),
            dma((2, 4)), dma((4,)), dma((2,)), dma((2, ny // 2)), dma((2, ny // 2)),
            dma(()), dma((ny // 2,)), dma(()), dma((ny // 2,)), dma(()), dma((ny,)), dma(()), dma(()),
        ],
        compiler_params=pltpu.CompilerParams(
            collective_id=1, has_side_effects=True, vmem_limit_bytes=limit
        ),
    )(query_act, key_act, value_act, grad_out, filter_taps, own, prev, back)
    *done, summed = pl.pallas_call(
        write_out,
        out_shape=[big] * 4 + [small],
        in_specs=[vmem] * 5,
        out_specs=[hbm] * 5,
        scratch_shapes=[dma((5,))],
        compiler_params=pltpu.CompilerParams(vmem_limit_bytes=2**20),
    )(*outs)
    return (*done, summed.T)


def solution(mesh):
    spread = P("dp", "ctx", None)
    return jax.shard_map(
        per_device, mesh=mesh, in_specs=(spread,) * 4 + (P(),),
        out_specs=(spread,) * 4 + (P(None, "ctx"),), check_vma=False,
    )
```

```python
import functools
import math

import jax
import jax.numpy as jnp
import ml_dtypes
import numpy as np
from jax import lax
from jax.experimental import pallas as pl
from jax.experimental.pallas import tpu as pltpu
from jax.sharding import PartitionSpec as P

MESH = pl.DeviceIdType.MESH
bf16 = jnp.bfloat16
f32 = jnp.float32
T = 128
F = 128
W = 256
NX = 4
VMEM_BYTES = 64929792
PIECES = 2
PIECES = 2
PIECES = 2
PIECES = 2


def split(matrix):
    hi = matrix.astype(ml_dtypes.bfloat16)
    lo = (matrix - hi.astype(np.float64)).astype(ml_dtypes.bfloat16)
    return hi, lo


def transforms():
    theta = np.pi * (2 * np.arange(F) + 1) / 256.0
    n = np.arange(T)

    def forward(shift):
        angle = theta[:, None] * (n + shift)[None, :]
        return np.concatenate([np.cos(angle), -np.sin(angle)], axis=0)

    own_hi, own_lo = split(forward(0))
    prev_hi, prev_lo = split(forward(-T))
    back_hi, back_lo = split(forward(0).T / F)
    return (
        np.concatenate([own_hi, own_lo], axis=1),
        np.concatenate([prev_hi, prev_lo], axis=1),
        np.concatenate([back_hi, back_hi, back_lo], axis=1),
    )


def kernel(
    nz, ny,
    q_hbm, k_hbm, v_hbm, g_hbm, h_hbm, own_hbm, prev_hbm, back_hbm,
    y_hbm, gq_hbm, gk_hbm, gv_hbm, gf_ref,
    q_ref, k_ref, v_ref, g_ref, h_ref, own_ref, prev_ref, back_ref,
    prev_kg, kg, halo, extra, spec, spec_h, early_sum, mates,
    part_x, recv_x, part_y, recv_y, part_z, recv_z,
    load_sem, const_sem, halo_send, halo_recv, late_recv, extra_send, extra_recv,
    send_x, sem_x, send_y, sem_y, send_z, sem_z,
):
    z = lax.axis_index("dp")
    c = lax.axis_index("ctx")
    nc = ny * 2 * NX
    yy = c // (2 * NX)
    x = (c // 2) % NX
    core = c % 2
    near = 1 - core
    nb = ny // 2
    half = nb * W
    right = {"dp": z, "ctx": lax.rem(c + 1, nc)}
    left = {"dp": z, "ctx": lax.rem(c + nc - 1, nc)}
    partner = {"dp": z, "ctx": c + 1 - 2 * core}
    far = {"dp": z, "ctx": lax.rem(c + 2 * core - 1 + nc, nc)}

    def at(y_to, x_to, core_to):
        return {"dp": z, "ctx": y_to * (2 * NX) + x_to * 2 + core_to}

    def at_x(d):
        return at(yy, lax.rem(x + d, NX), core)

    def at_z(d):
        return {"dp": lax.rem(z + d, nz), "ctx": c}

    def load(s):
        cols = pl.ds(pl.multiple_of(s * half, half), half)
        return [
            pltpu.make_async_copy(src.at[0, :, cols], dst.at[s], load_sem.at[s, i])
            for i, (src, dst) in enumerate(
                [(k_hbm, k_ref), (v_hbm, v_ref), (g_hbm, g_ref), (q_hbm, q_ref)]
            )
        ]

    for copy in load(near):
        copy.start()
    constants = [
        pltpu.make_async_copy(src, dst, const_sem.at[i])
        for i, (src, dst) in enumerate(
            [(own_hbm, own_ref), (h_hbm, h_ref), (prev_hbm, prev_ref), (back_hbm, back_ref)]
        )
    ]
    barrier = pltpu.get_barrier_semaphore()

    def greet(device):
        pl.semaphore_signal(barrier, inc=1, device_id=device, device_id_type=MESH)

    source_core = yy // nb
    own_source = source_core == core
    for d in sorted(range(1, nz), key=lambda d: abs(d - nz // 2)):
        greet(at_z(d))
    greet(left)
    greet(right)
    for d in sorted(range(ny), key=lambda d: abs(d - ny // 2)):
        ys = lax.rem(yy + d, ny)
        if d:
            greet(at(ys, x, source_core))
        else:
            @pl.when(jnp.logical_not(own_source))
            def _():
                greet(at(ys, x, source_core))
    for d in (2, 1, 3):
        greet(at_x(d))

    def products(s):
        for j in range(nb):
            cols = slice(j * W, (j + 1) * W)
            b = s * nb + j
            kg[0, b] = (k_ref[s, :, cols].astype(f32) * v_ref[s, :, cols].astype(f32)).astype(bf16)
            kg[1, b] = (g_ref[s, :, cols].astype(f32) * q_ref[s, :, cols].astype(f32)).astype(bf16)

    for copy in load(near):
        copy.wait()
    for copy in load(core):
        copy.start()
    for copy in constants:
        copy.start()
    products(near)
    pl.semaphore_wait(barrier, 2 + (NX - 1) + (nz - 1) + jnp.where(own_source, ny - 1, ny))

    def halo_copy(array, b, device):
        return pltpu.make_async_remote_copy(
            src_ref=kg.at[array, b], dst_ref=halo.at[array, b],
            send_sem=halo_send.at[array], recv_sem=halo_recv.at[array, b % nb],
            device_id=device, device_id_type=MESH,
        )

    def late_copy(array, b, device):
        return pltpu.make_async_remote_copy(
            src_ref=kg.at[array, b], dst_ref=halo.at[array, b],
            send_sem=halo_send.at[array], recv_sem=late_recv.at[array, b % nb],
            device_id=device, device_id_type=MESH,
        )

    def send_late(first_block, last_block):
        for j in range(first_block, last_block):
            late_copy(near, core * nb + j, far).start()

    def send_near():
        for j in range(nb):
            late_copy(core, core * nb + j, partner).start()

    turn = x == jnp.where(core == 1, NX - 1, 0)

    def extra_copy(j):
        return pltpu.make_async_remote_copy(
            src_ref=kg.at[near, near * nb + j], dst_ref=extra.at[j],
            send_sem=extra_send, recv_sem=extra_recv.at[j],
            device_id=partner, device_id_type=MESH,
        )

    for j in range(nb):
        halo_copy(near, near * nb + j, far).start()
    for j in range(nb):
        halo_copy(core, near * nb + j, partner).start()
        extra_copy(j).start()

    for copy in load(core):
        copy.wait()
    products(core)

    for copy in constants:
        copy.wait()
    prev_kg[0] = prev_ref[...] * jnp.where(c > 0, 1.0, 0.0).astype(bf16)
    prev_kg[1] = prev_ref[...] * jnp.where(c < nc - 1, -1.0, 0.0).astype(bf16)

    def forward(matrix, value):
        return jnp.dot(
            matrix, jnp.concatenate([value, value], axis=0), preferred_element_type=f32
        )

    def own_spectra(s):
        def step(j, carry):
            b = s * nb + j
            spec[0, b] = forward(own_ref[...], kg[0, b])
            spec[1, b] = forward(own_ref[...], kg[1, b])
            return carry

        lax.fori_loop(0, nb, step, 0)

    def tap_spectra(s):
        def step(j, carry):
            b = s * nb + j
            taps = h_ref[:, pl.ds(pl.multiple_of(b * W, W), W)]
            spec_h[b] = forward(own_ref[...], taps)
            return carry

        lax.fori_loop(0, nb, step, 0)

    own_spectra(core)

    def times(a, b):
        ar, ai, br, bi = a[:F], a[F:], b[:F], b[F:]
        return ar * br - ai * bi, ar * bi + ai * br

    def times_conj(a, b):
        ar, ai, br, bi = a[:F], a[F:], b[:F], b[F:]
        return ar * br + ai * bi, ai * br - ar * bi

    def inverse(re, im):
        value = jnp.concatenate([re, im], axis=0)
        hi = value.astype(bf16)
        lo = (value - hi.astype(f32)).astype(bf16)
        return jnp.dot(
            back_ref[...], jnp.concatenate([hi, lo, hi], axis=0), preferred_element_type=f32
        )

    first = core == 0

    def early_terms(j, carry):
        b = core * nb + j
        halo_copy(1 - core, b, partner).wait_recv()
        extra_copy(j).wait_recv()
        fast = forward(prev_kg[near], halo[near, b])
        other = forward(prev_ref[...], extra[j])
        own_k = spec[0, b]
        own_g = spec[1, b]
        spec[near, b] = spec[near, b] + fast
        re0, im0 = times_conj(jnp.where(first, own_g + fast, own_g), jnp.where(first, own_k, own_k + fast))
        re1, im1 = times_conj(jnp.where(first, -fast, other), jnp.where(first, other, fast))
        mates[j] = jnp.where(first, own_g, own_k)
        early_sum[j, :F] = re0 + re1
        early_sum[j, F:] = im0 + im1
        return carry

    lax.fori_loop(0, nb, early_terms, 0)

    def gradient(j, carry):
        b = core * nb + j
        halo_copy(core, b, partner).wait_recv()
        slow = forward(prev_kg[core], halo[core, b])
        own = spec[core, b]
        spec[core, b] = own + slow
        mate = mates[j]
        re, im = times_conj(jnp.where(first, mate, slow), jnp.where(first, slow, mate))
        value = inverse(early_sum[j, :F] + re, early_sum[j, F:] + im)
        part_x[j] = jnp.transpose(value).astype(bf16).reshape(NX, W // NX, T)
        for d in (2, 1, 3):
            pltpu.make_async_remote_copy(
                src_ref=part_x.at[j, lax.rem(x + d, NX)], dst_ref=recv_x.at[j, d - 1],
                send_sem=send_x, recv_sem=sem_x.at[j], device_id=at_x(d), device_id_type=MESH,
            ).start()
        return carry

    lax.fori_loop(0, nb, gradient, 0)
    @pl.when(turn)
    def _():
        send_late(0, nb // 2)


    def outputs(s, first_block, last_block):
        def step(j, carry):
            b = s * nb + j
            if s is near:
                late_copy(0, b, right).wait_recv()
                late_copy(1, b, left).wait_recv()
            k_all = spec[0, b]
            g_all = spec[1, b]
            if s is near:
                k_all += forward(prev_kg[0], halo[0, b])
                g_all += forward(prev_kg[1], halo[1, b])
            taps = spec_h[b]
            cols = pl.ds(pl.multiple_of(j * W, W), W)
            full = pl.ds(pl.multiple_of(b * W, W), W)
            m = inverse(*times(k_all, taps))
            y_hbm[0, :, full] = (q_ref[s, :, cols].astype(f32) * m).astype(bf16)
            gq_hbm[0, :, full] = (g_ref[s, :, cols].astype(f32) * m).astype(bf16)
            m = inverse(*times_conj(g_all, taps))
            gk_hbm[0, :, full] = (v_ref[s, :, cols].astype(f32) * m).astype(bf16)
            gv_hbm[0, :, full] = (k_ref[s, :, cols].astype(f32) * m).astype(bf16)
            return carry

        lax.fori_loop(first_block, last_block, step, 0)

    def landed(ref, sem):
        pltpu.make_async_copy(ref, ref, sem).wait()

    own_spectra(near)

    for j in range(nb):
        landed(recv_x.at[j], sem_x.at[j])
        total = part_x[j, x].astype(f32)
        for d in range(NX - 1):
            total += recv_x[j, d].astype(f32)
        part_y[j] = total.astype(bf16).reshape(2, W // NX // 2, T)
        for core_to in range(2):
            mine = jnp.logical_and(jnp.logical_and(own_source, yy == core * nb + j), core == core_to)

            @pl.when(jnp.logical_not(mine))
            def _():
                pltpu.make_async_remote_copy(
                    src_ref=part_y.at[j, core_to], dst_ref=recv_y.at[yy],
                    send_sem=send_y, recv_sem=sem_y.at[yy],
                    device_id=at(core * nb + j, x, core_to), device_id_type=MESH,
                ).start()

            @pl.when(mine)
            def _():
                recv_y[yy] = part_y[j, core_to]

    send_near()
    @pl.when(jnp.logical_not(turn))
    def _():
        send_late(0, nb)

    tap_spectra(core)
    tap_spectra(near)
    outputs(core, 0, nb)

    @pl.when(turn)
    def _():
        send_late(nb // 2, nb)


    for ys in range(ny):
        @pl.when(jnp.logical_not(jnp.logical_and(ys == yy, own_source)))
        def _():
            landed(recv_y.at[ys], sem_y.at[ys])
    total = recv_y[0].astype(f32)
    for ys in range(1, ny):
        total += recv_y[ys].astype(f32)
    part_z[...] = total.astype(bf16)
    for d in sorted(range(1, nz), key=lambda d: abs(d - nz // 2)):
        pltpu.make_async_remote_copy(
            src_ref=part_z, dst_ref=recv_z.at[d - 1], send_sem=send_z, recv_sem=sem_z,
            device_id=at_z(d), device_id_type=MESH,
        ).start()

    outputs(near, 0, nb)

    landed(kg.at[0], halo_send.at[0])
    landed(kg.at[1], halo_send.at[1])
    landed(extra, extra_send)
    landed(recv_x, send_x)
    landed(recv_y.at[pl.ds(0, ny - 1)], send_y)

    @pl.when(jnp.logical_not(own_source))
    def _():
        landed(recv_y.at[ny - 1], send_y)

    landed(recv_z, sem_z)
    total = part_z[...].astype(f32)
    for d in range(nz - 1):
        total += recv_z[d].astype(f32)
    gf_ref[...] = total * (1.0 / math.sqrt(T * nc * nz))

    landed(recv_z, send_z)


def write_out(*refs):
    sem = refs[10]
    copies = [pltpu.make_async_copy(refs[i], refs[5 + i], sem.at[i]) for i in range(5)]
    for copy in copies:
        copy.start()
    for copy in copies:
        copy.wait()


def per_device(query_act, key_act, value_act, grad_out, filter_taps):
    channels = filter_taps.shape[1]
    ny = channels // W
    nz = lax.axis_size("dp")
    own, prev, back = transforms()
    big = jax.ShapeDtypeStruct((1, T, channels), bf16)
    half = channels // 2
    cols = W // NX // 2
    small = jax.ShapeDtypeStruct((cols, T), f32)
    hbm = pl.BlockSpec(memory_space=pl.ANY)
    vmem = pl.BlockSpec(memory_space=pltpu.VMEM)
    dma = pltpu.SemaphoreType.DMA
    limit = VMEM_BYTES
    outs = pl.pallas_call(
        functools.partial(kernel, nz, ny),
        out_shape=[pltpu.VMEM(big.shape, bf16)] * 4 + [pltpu.VMEM(small.shape, f32)],
        in_specs=[hbm] * 8,
        out_specs=[vmem] * 5,
        scratch_shapes=[
            *[pltpu.VMEM((2, T, half), bf16)] * 4,
            pltpu.VMEM((T, channels), bf16),
            pltpu.VMEM((2 * F, 2 * T), bf16),
            pltpu.VMEM((2 * F, 2 * T), bf16),
            pltpu.VMEM((T, 6 * F), bf16),
            pltpu.VMEM((2, 2 * F, 2 * T), bf16),
            pltpu.VMEM((2, ny, T, W), bf16),
            pltpu.VMEM((2, ny, T, W), bf16),
            pltpu.VMEM((ny // 2, T, W), bf16),
            pltpu.VMEM((2, ny, 2 * F, W), f32),
            pltpu.VMEM((ny, 2 * F, W), f32),
            pltpu.VMEM((ny // 2, 2 * F, W), f32),
            pltpu.VMEM((ny // 2, 2 * F, W), f32),
            pltpu.VMEM((ny // 2, NX, W // NX, T), bf16),
            pltpu.VMEM((ny // 2, NX - 1, W // NX, T), bf16),
            pltpu.VMEM((ny // 2, 2, cols, T), bf16),
            pltpu.VMEM((ny, cols, T), bf16),
            pltpu.VMEM((cols, T), bf16),
            pltpu.VMEM((nz - 1, cols, T), bf16),
            dma((2, 4)), dma((4,)), dma((2,)), dma((2, ny // 2)), dma((2, ny // 2)),
            dma(()), dma((ny // 2,)), dma(()), dma((ny // 2,)), dma(()), dma((ny,)), dma(()), dma(()),
        ],
        compiler_params=pltpu.CompilerParams(
            collective_id=1, has_side_effects=True, vmem_limit_bytes=limit
        ),
    )(query_act, key_act, value_act, grad_out, filter_taps, own, prev, back)
    *done, summed = pl.pallas_call(
        write_out,
        out_shape=[big] * 4 + [small],
        in_specs=[vmem] * 5,
        out_specs=[hbm] * 5,
        scratch_shapes=[dma((5,))],
        compiler_params=pltpu.CompilerParams(vmem_limit_bytes=2**20),
    )(*outs)
    return (*done, summed.T)


def solution(mesh):
    spread = P("dp", "ctx", None)
    return jax.shard_map(
        per_device, mesh=mesh, in_specs=(spread,) * 4 + (P(),),
        out_specs=(spread,) * 4 + (P(None, "ctx"),), check_vma=False,
    )
```

```python
import functools
import math

import jax
import jax.numpy as jnp
import ml_dtypes
import numpy as np
from jax import lax
from jax.experimental import pallas as pl
from jax.experimental.pallas import tpu as pltpu
from jax.sharding import PartitionSpec as P

MESH = pl.DeviceIdType.MESH
bf16 = jnp.bfloat16
f32 = jnp.float32
T = 128
F = 128
W = 256
NX = 4
VMEM_BYTES = 64929792
PIECES = 2
PIECES = 2
PIECES = 2
PIECES = 2


def split(matrix):
    hi = matrix.astype(ml_dtypes.bfloat16)
    lo = (matrix - hi.astype(np.float64)).astype(ml_dtypes.bfloat16)
    return hi, lo


def transforms():
    theta = np.pi * (2 * np.arange(F) + 1) / 256.0
    n = np.arange(T)

    def forward(shift):
        angle = theta[:, None] * (n + shift)[None, :]
        return np.concatenate([np.cos(angle), -np.sin(angle)], axis=0)

    own_hi, own_lo = split(forward(0))
    prev_hi, prev_lo = split(forward(-T))
    back_hi, back_lo = split(forward(0).T / F)
    return (
        np.concatenate([own_hi, own_lo], axis=1),
        np.concatenate([prev_hi, prev_lo], axis=1),
        np.concatenate([back_hi, back_hi, back_lo], axis=1),
    )


def kernel(
    nz, ny,
    q_hbm, k_hbm, v_hbm, g_hbm, h_hbm, own_hbm, prev_hbm, back_hbm,
    y_hbm, gq_hbm, gk_hbm, gv_hbm, gf_ref,
    q_ref, k_ref, v_ref, g_ref, h_ref, own_ref, prev_ref, back_ref,
    prev_kg, kg, halo, extra, spec, spec_h, early_sum, mates,
    part_x, recv_x, part_y, recv_y, part_z, recv_z,
    load_sem, const_sem, halo_send, halo_recv, late_recv, extra_send, extra_recv,
    send_x, sem_x, send_y, sem_y, send_z, sem_z,
):
    z = lax.axis_index("dp")
    c = lax.axis_index("ctx")
    nc = ny * 2 * NX
    yy = c // (2 * NX)
    x = (c // 2) % NX
    core = c % 2
    near = 1 - core
    nb = ny // 2
    half = nb * W
    right = {"dp": z, "ctx": lax.rem(c + 1, nc)}
    left = {"dp": z, "ctx": lax.rem(c + nc - 1, nc)}
    partner = {"dp": z, "ctx": c + 1 - 2 * core}
    far = {"dp": z, "ctx": lax.rem(c + 2 * core - 1 + nc, nc)}

    def at(y_to, x_to, core_to):
        return {"dp": z, "ctx": y_to * (2 * NX) + x_to * 2 + core_to}

    def at_x(d):
        return at(yy, lax.rem(x + d, NX), core)

    def at_z(d):
        return {"dp": lax.rem(z + d, nz), "ctx": c}

    def load(s):
        cols = pl.ds(pl.multiple_of(s * half, half), half)
        return [
            pltpu.make_async_copy(src.at[0, :, cols], dst.at[s], load_sem.at[s, i])
            for i, (src, dst) in enumerate(
                [(k_hbm, k_ref), (v_hbm, v_ref), (g_hbm, g_ref), (q_hbm, q_ref)]
            )
        ]

    for copy in load(near):
        copy.start()
    constants = [
        pltpu.make_async_copy(src, dst, const_sem.at[i])
        for i, (src, dst) in enumerate(
            [(own_hbm, own_ref), (h_hbm, h_ref), (prev_hbm, prev_ref), (back_hbm, back_ref)]
        )
    ]
    barrier = pltpu.get_barrier_semaphore()

    def greet(device):
        pl.semaphore_signal(barrier, inc=1, device_id=device, device_id_type=MESH)

    source_core = yy // nb
    own_source = source_core == core
    for d in sorted(range(1, nz), key=lambda d: abs(d - nz // 2)):
        greet(at_z(d))
    greet(left)
    greet(right)
    for d in sorted(range(ny), key=lambda d: abs(d - ny // 2)):
        ys = lax.rem(yy + d, ny)
        if d:
            greet(at(ys, x, source_core))
        else:
            @pl.when(jnp.logical_not(own_source))
            def _():
                greet(at(ys, x, source_core))
    for d in (2, 1, 3):
        greet(at_x(d))

    def products(s):
        for j in range(nb):
            cols = slice(j * W, (j + 1) * W)
            b = s * nb + j
            kg[0, b] = (k_ref[s, :, cols].astype(f32) * v_ref[s, :, cols].astype(f32)).astype(bf16)
            kg[1, b] = (g_ref[s, :, cols].astype(f32) * q_ref[s, :, cols].astype(f32)).astype(bf16)

    for copy in load(near):
        copy.wait()
    for copy in load(core):
        copy.start()
    for copy in constants:
        copy.start()
    products(near)
    pl.semaphore_wait(barrier, 2 + (NX - 1) + (nz - 1) + jnp.where(own_source, ny - 1, ny))

    def halo_copy(array, b, device):
        return pltpu.make_async_remote_copy(
            src_ref=kg.at[array, b], dst_ref=halo.at[array, b],
            send_sem=halo_send.at[array], recv_sem=halo_recv.at[array, b % nb],
            device_id=device, device_id_type=MESH,
        )

    def half_copy(array, b, part, device):
        lanes = pl.ds(part * (W // 2), W // 2)
        return pltpu.make_async_remote_copy(
            src_ref=kg.at[array, b, :, lanes], dst_ref=halo.at[array, b, :, lanes],
            send_sem=halo_send.at[array], recv_sem=halo_recv.at[array, nb - 1 + part],
            device_id=device, device_id_type=MESH,
        )

    def late_copy(array, b, device):
        return pltpu.make_async_remote_copy(
            src_ref=kg.at[array, b], dst_ref=halo.at[array, b],
            send_sem=halo_send.at[array], recv_sem=late_recv.at[array, b % nb],
            device_id=device, device_id_type=MESH,
        )

    def send_late(first_block, last_block):
        for j in range(first_block, last_block):
            late_copy(near, core * nb + j, far).start()

    def send_near():
        for j in range(nb):
            late_copy(core, core * nb + j, partner).start()

    turn = x == jnp.where(core == 1, NX - 1, 0)

    def extra_copy(j):
        return pltpu.make_async_remote_copy(
            src_ref=kg.at[near, near * nb + j], dst_ref=extra.at[j],
            send_sem=extra_send, recv_sem=extra_recv.at[j],
            device_id=partner, device_id_type=MESH,
        )

    for j in range(nb - 1):
        halo_copy(near, near * nb + j, far).start()
    for part in range(2):
        half_copy(near, near * nb + nb - 1, part, far).start()
    for j in range(nb):
        halo_copy(core, near * nb + j, partner).start()
        extra_copy(j).start()

    for copy in load(core):
        copy.wait()
    products(core)

    for copy in constants:
        copy.wait()
    prev_kg[0] = prev_ref[...] * jnp.where(c > 0, 1.0, 0.0).astype(bf16)
    prev_kg[1] = prev_ref[...] * jnp.where(c < nc - 1, -1.0, 0.0).astype(bf16)

    def forward(matrix, value):
        return jnp.dot(
            matrix, jnp.concatenate([value, value], axis=0), preferred_element_type=f32
        )

    def own_spectra(s):
        def step(j, carry):
            b = s * nb + j
            spec[0, b] = forward(own_ref[...], kg[0, b])
            spec[1, b] = forward(own_ref[...], kg[1, b])
            return carry

        lax.fori_loop(0, nb, step, 0)

    def tap_spectra(s):
        def step(j, carry):
            b = s * nb + j
            taps = h_ref[:, pl.ds(pl.multiple_of(b * W, W), W)]
            spec_h[b] = forward(own_ref[...], taps)
            return carry

        lax.fori_loop(0, nb, step, 0)

    own_spectra(core)

    def times(a, b):
        ar, ai, br, bi = a[:F], a[F:], b[:F], b[F:]
        return ar * br - ai * bi, ar * bi + ai * br

    def times_conj(a, b):
        ar, ai, br, bi = a[:F], a[F:], b[:F], b[F:]
        return ar * br + ai * bi, ai * br - ar * bi

    def inverse(re, im):
        value = jnp.concatenate([re, im], axis=0)
        hi = value.astype(bf16)
        lo = (value - hi.astype(f32)).astype(bf16)
        return jnp.dot(
            back_ref[...], jnp.concatenate([hi, lo, hi], axis=0), preferred_element_type=f32
        )

    first = core == 0

    def early_terms(j, carry):
        b = core * nb + j
        halo_copy(1 - core, b, partner).wait_recv()
        extra_copy(j).wait_recv()
        fast = forward(prev_kg[near], halo[near, b])
        other = forward(prev_ref[...], extra[j])
        own_k = spec[0, b]
        own_g = spec[1, b]
        spec[near, b] = spec[near, b] + fast
        re0, im0 = times_conj(jnp.where(first, own_g + fast, own_g), jnp.where(first, own_k, own_k + fast))
        re1, im1 = times_conj(jnp.where(first, -fast, other), jnp.where(first, other, fast))
        mates[j] = jnp.where(first, own_g, own_k)
        early_sum[j, :F] = re0 + re1
        early_sum[j, F:] = im0 + im1
        return carry

    lax.fori_loop(0, nb, early_terms, 0)

    def slow_terms(j, lanes):
        b = core * nb + j
        slow = forward(prev_kg[core], halo[core, b, :, lanes])
        spec[core, b, :, lanes] = spec[core, b, :, lanes] + slow
        mate = mates[j, :, lanes]
        re, im = times_conj(jnp.where(first, mate, slow), jnp.where(first, slow, mate))
        value = inverse(early_sum[j, :F, lanes] + re, early_sum[j, F:, lanes] + im)
        return jnp.transpose(value).astype(bf16)

    def send_block(j, d):
        pltpu.make_async_remote_copy(
            src_ref=part_x.at[j, lax.rem(x + d, NX)], dst_ref=recv_x.at[j, d - 1],
            send_sem=send_x, recv_sem=sem_x.at[j], device_id=at_x(d), device_id_type=MESH,
        ).start()

    def gradient(j, carry):
        halo_copy(core, core * nb + j, partner).wait_recv()
        part_x[j] = slow_terms(j, slice(None)).reshape(NX, W // NX, T)
        for d in (2, 1, 3):
            send_block(j, d)
        return carry

    lax.fori_loop(0, nb - 1, gradient, 0)
    for part in range(2):
        half_copy(core, core * nb + nb - 1, part, partner).wait_recv()
        lanes = slice(part * (W // 2), (part + 1) * (W // 2))
        owners = slice(part * (NX // 2), (part + 1) * (NX // 2))
        part_x[nb - 1, owners] = slow_terms(nb - 1, lanes).reshape(NX // 2, W // NX, T)
        for d in (2, 1, 3):
            @pl.when(lax.rem(x + d, NX) // (NX // 2) == part)
            def _():
                send_block(nb - 1, d)

    @pl.when(turn)
    def _():
        send_late(0, nb // 2)


    def outputs(s, first_block, last_block):
        def step(j, carry):
            b = s * nb + j
            if s is near:
                late_copy(0, b, right).wait_recv()
                late_copy(1, b, left).wait_recv()
            k_all = spec[0, b]
            g_all = spec[1, b]
            if s is near:
                k_all += forward(prev_kg[0], halo[0, b])
                g_all += forward(prev_kg[1], halo[1, b])
            taps = spec_h[b]
            cols = pl.ds(pl.multiple_of(j * W, W), W)
            full = pl.ds(pl.multiple_of(b * W, W), W)
            m = inverse(*times(k_all, taps))
            y_hbm[0, :, full] = (q_ref[s, :, cols].astype(f32) * m).astype(bf16)
            gq_hbm[0, :, full] = (g_ref[s, :, cols].astype(f32) * m).astype(bf16)
            m = inverse(*times_conj(g_all, taps))
            gk_hbm[0, :, full] = (v_ref[s, :, cols].astype(f32) * m).astype(bf16)
            gv_hbm[0, :, full] = (k_ref[s, :, cols].astype(f32) * m).astype(bf16)
            return carry

        lax.fori_loop(first_block, last_block, step, 0)

    def landed(ref, sem):
        pltpu.make_async_copy(ref, ref, sem).wait()

    own_spectra(near)

    for j in range(nb):
        landed(recv_x.at[j], sem_x.at[j])
        total = part_x[j, x].astype(f32)
        for d in range(NX - 1):
            total += recv_x[j, d].astype(f32)
        part_y[j] = total.astype(bf16).reshape(2, W // NX // 2, T)
        for core_to in range(2):
            mine = jnp.logical_and(jnp.logical_and(own_source, yy == core * nb + j), core == core_to)

            @pl.when(jnp.logical_not(mine))
            def _():
                pltpu.make_async_remote_copy(
                    src_ref=part_y.at[j, core_to], dst_ref=recv_y.at[yy],
                    send_sem=send_y, recv_sem=sem_y.at[yy],
                    device_id=at(core * nb + j, x, core_to), device_id_type=MESH,
                ).start()

            @pl.when(mine)
            def _():
                recv_y[yy] = part_y[j, core_to]

    send_near()
    @pl.when(jnp.logical_not(turn))
    def _():
        send_late(0, nb)

    tap_spectra(core)
    tap_spectra(near)
    outputs(core, 0, nb)

    @pl.when(turn)
    def _():
        send_late(nb // 2, nb)


    for ys in range(ny):
        @pl.when(jnp.logical_not(jnp.logical_and(ys == yy, own_source)))
        def _():
            landed(recv_y.at[ys], sem_y.at[ys])
    total = recv_y[0].astype(f32)
    for ys in range(1, ny):
        total += recv_y[ys].astype(f32)
    part_z[...] = total.astype(bf16)
    for d in sorted(range(1, nz), key=lambda d: abs(d - nz // 2)):
        pltpu.make_async_remote_copy(
            src_ref=part_z, dst_ref=recv_z.at[d - 1], send_sem=send_z, recv_sem=sem_z,
            device_id=at_z(d), device_id_type=MESH,
        ).start()

    outputs(near, 0, nb)

    landed(kg.at[0], halo_send.at[0])
    landed(kg.at[1], halo_send.at[1])
    landed(extra, extra_send)
    landed(recv_x, send_x)
    landed(recv_y.at[pl.ds(0, ny - 1)], send_y)

    @pl.when(jnp.logical_not(own_source))
    def _():
        landed(recv_y.at[ny - 1], send_y)

    landed(recv_z, sem_z)
    total = part_z[...].astype(f32)
    for d in range(nz - 1):
        total += recv_z[d].astype(f32)
    gf_ref[...] = total * (1.0 / math.sqrt(T * nc * nz))

    landed(recv_z, send_z)


def write_out(*refs):
    sem = refs[10]
    copies = [pltpu.make_async_copy(refs[i], refs[5 + i], sem.at[i]) for i in range(5)]
    for copy in copies:
        copy.start()
    for copy in copies:
        copy.wait()


def per_device(query_act, key_act, value_act, grad_out, filter_taps):
    channels = filter_taps.shape[1]
    ny = channels // W
    nz = lax.axis_size("dp")
    own, prev, back = transforms()
    big = jax.ShapeDtypeStruct((1, T, channels), bf16)
    half = channels // 2
    cols = W // NX // 2
    small = jax.ShapeDtypeStruct((cols, T), f32)
    hbm = pl.BlockSpec(memory_space=pl.ANY)
    vmem = pl.BlockSpec(memory_space=pltpu.VMEM)
    dma = pltpu.SemaphoreType.DMA
    limit = VMEM_BYTES
    outs = pl.pallas_call(
        functools.partial(kernel, nz, ny),
        out_shape=[pltpu.VMEM(big.shape, bf16)] * 4 + [pltpu.VMEM(small.shape, f32)],
        in_specs=[hbm] * 8,
        out_specs=[vmem] * 5,
        scratch_shapes=[
            *[pltpu.VMEM((2, T, half), bf16)] * 4,
            pltpu.VMEM((T, channels), bf16),
            pltpu.VMEM((2 * F, 2 * T), bf16),
            pltpu.VMEM((2 * F, 2 * T), bf16),
            pltpu.VMEM((T, 6 * F), bf16),
            pltpu.VMEM((2, 2 * F, 2 * T), bf16),
            pltpu.VMEM((2, ny, T, W), bf16),
            pltpu.VMEM((2, ny, T, W), bf16),
            pltpu.VMEM((ny // 2, T, W), bf16),
            pltpu.VMEM((2, ny, 2 * F, W), f32),
            pltpu.VMEM((ny, 2 * F, W), f32),
            pltpu.VMEM((ny // 2, 2 * F, W), f32),
            pltpu.VMEM((ny // 2, 2 * F, W), f32),
            pltpu.VMEM((ny // 2, NX, W // NX, T), bf16),
            pltpu.VMEM((ny // 2, NX - 1, W // NX, T), bf16),
            pltpu.VMEM((ny // 2, 2, cols, T), bf16),
            pltpu.VMEM((ny, cols, T), bf16),
            pltpu.VMEM((cols, T), bf16),
            pltpu.VMEM((nz - 1, cols, T), bf16),
            dma((2, 4)), dma((4,)), dma((2,)), dma((2, ny // 2 + 1)), dma((2, ny // 2)),
            dma(()), dma((ny // 2,)), dma(()), dma((ny // 2,)), dma(()), dma((ny,)), dma(()), dma(()),
        ],
        compiler_params=pltpu.CompilerParams(
            collective_id=1, has_side_effects=True, vmem_limit_bytes=limit
        ),
    )(query_act, key_act, value_act, grad_out, filter_taps, own, prev, back)
    *done, summed = pl.pallas_call(
        write_out,
        out_shape=[big] * 4 + [small],
        in_specs=[vmem] * 5,
        out_specs=[hbm] * 5,
        scratch_shapes=[dma((5,))],
        compiler_params=pltpu.CompilerParams(vmem_limit_bytes=2**20),
    )(*outs)
    return (*done, summed.T)


def solution(mesh):
    spread = P("dp", "ctx", None)
    return jax.shard_map(
        per_device, mesh=mesh, in_specs=(spread,) * 4 + (P(),),
        out_specs=(spread,) * 4 + (P(None, "ctx"),), check_vma=False,
    )
```

```python
import functools
import math

import jax
import jax.numpy as jnp
import ml_dtypes
import numpy as np
from jax import lax
from jax.experimental import pallas as pl
from jax.experimental.pallas import tpu as pltpu
from jax.sharding import PartitionSpec as P

MESH = pl.DeviceIdType.MESH
bf16 = jnp.bfloat16
f32 = jnp.float32
T = 128
F = 128
W = 256
NX = 4
VMEM_BYTES = 64929792
PIECES = 2
PIECES = 2
PIECES = 2
PIECES = 2


def split(matrix):
    hi = matrix.astype(ml_dtypes.bfloat16)
    lo = (matrix - hi.astype(np.float64)).astype(ml_dtypes.bfloat16)
    return hi, lo


def transforms():
    theta = np.pi * (2 * np.arange(F) + 1) / 256.0
    n = np.arange(T)

    def forward(shift):
        angle = theta[:, None] * (n + shift)[None, :]
        return np.concatenate([np.cos(angle), -np.sin(angle)], axis=0)

    own_hi, own_lo = split(forward(0))
    prev_hi, prev_lo = split(forward(-T))
    back_hi, back_lo = split(forward(0).T / F)
    return (
        np.concatenate([own_hi, own_lo], axis=1),
        np.concatenate([prev_hi, prev_lo], axis=1),
        np.concatenate([back_hi, back_hi, back_lo], axis=1),
    )


def kernel(
    nz, ny,
    q_hbm, k_hbm, v_hbm, g_hbm, h_hbm, own_hbm, prev_hbm, back_hbm,
    y_hbm, gq_hbm, gk_hbm, gv_hbm, gf_ref,
    q_ref, k_ref, v_ref, g_ref, h_ref, own_ref, prev_ref, back_ref,
    prev_kg, kg, halo, extra, spec, spec_h, early_sum, mates,
    part_x, recv_x, part_y, recv_y, part_z, recv_z,
    load_sem, const_sem, halo_send, halo_recv, late_recv, extra_send, extra_recv,
    send_x, sem_x, send_y, sem_y, send_z, sem_z,
):
    z = lax.axis_index("dp")
    c = lax.axis_index("ctx")
    nc = ny * 2 * NX
    yy = c // (2 * NX)
    x = (c // 2) % NX
    core = c % 2
    near = 1 - core
    nb = ny // 2
    half = nb * W
    right = {"dp": z, "ctx": lax.rem(c + 1, nc)}
    left = {"dp": z, "ctx": lax.rem(c + nc - 1, nc)}
    partner = {"dp": z, "ctx": c + 1 - 2 * core}
    far = {"dp": z, "ctx": lax.rem(c + 2 * core - 1 + nc, nc)}

    def at(y_to, x_to, core_to):
        return {"dp": z, "ctx": y_to * (2 * NX) + x_to * 2 + core_to}

    def at_x(d):
        return at(yy, lax.rem(x + d, NX), core)

    def at_z(d):
        return {"dp": lax.rem(z + d, nz), "ctx": c}

    def load(s):
        cols = pl.ds(pl.multiple_of(s * half, half), half)
        return [
            pltpu.make_async_copy(src.at[0, :, cols], dst.at[s], load_sem.at[s, i])
            for i, (src, dst) in enumerate(
                [(k_hbm, k_ref), (v_hbm, v_ref), (g_hbm, g_ref), (q_hbm, q_ref)]
            )
        ]

    for copy in load(near):
        copy.start()
    constants = [
        pltpu.make_async_copy(src, dst, const_sem.at[i])
        for i, (src, dst) in enumerate(
            [(own_hbm, own_ref), (h_hbm, h_ref), (prev_hbm, prev_ref), (back_hbm, back_ref)]
        )
    ]
    barrier = pltpu.get_barrier_semaphore()

    def greet(device):
        pl.semaphore_signal(barrier, inc=1, device_id=device, device_id_type=MESH)

    source_core = yy // nb
    own_source = source_core == core
    for d in sorted(range(1, nz), key=lambda d: abs(d - nz // 2)):
        greet(at_z(d))
    greet(left)
    greet(right)
    for d in sorted(range(ny), key=lambda d: abs(d - ny // 2)):
        ys = lax.rem(yy + d, ny)
        if d:
            greet(at(ys, x, source_core))
        else:
            @pl.when(jnp.logical_not(own_source))
            def _():
                greet(at(ys, x, source_core))
    for d in (2, 1, 3):
        greet(at_x(d))

    def products(s):
        for j in range(nb):
            cols = slice(j * W, (j + 1) * W)
            b = s * nb + j
            kg[0, b] = (k_ref[s, :, cols].astype(f32) * v_ref[s, :, cols].astype(f32)).astype(bf16)
            kg[1, b] = (g_ref[s, :, cols].astype(f32) * q_ref[s, :, cols].astype(f32)).astype(bf16)

    for copy in load(near):
        copy.wait()
    for copy in load(core):
        copy.start()
    for copy in constants:
        copy.start()
    products(near)
    pl.semaphore_wait(barrier, 2 + (NX - 1) + (nz - 1) + jnp.where(own_source, ny - 1, ny))

    def halo_copy(array, b, device):
        return pltpu.make_async_remote_copy(
            src_ref=kg.at[array, b], dst_ref=halo.at[array, b],
            send_sem=halo_send.at[array], recv_sem=halo_recv.at[array, b % nb],
            device_id=device, device_id_type=MESH,
        )

    def late_copy(array, b, device):
        return pltpu.make_async_remote_copy(
            src_ref=kg.at[array, b], dst_ref=halo.at[array, b],
            send_sem=halo_send.at[array], recv_sem=late_recv.at[array, b % nb],
            device_id=device, device_id_type=MESH,
        )

    def send_late(first_block, last_block):
        for j in range(first_block, last_block):
            late_copy(near, core * nb + j, far).start()

    def send_near():
        for j in range(nb):
            late_copy(core, core * nb + j, partner).start()

    turn = x == jnp.where(core == 1, NX - 1, 0)

    def extra_copy(j):
        return pltpu.make_async_remote_copy(
            src_ref=kg.at[near, near * nb + j], dst_ref=extra.at[j],
            send_sem=extra_send, recv_sem=extra_recv.at[j],
            device_id=partner, device_id_type=MESH,
        )

    for j in range(nb):
        halo_copy(near, near * nb + j, far).start()
    for j in range(nb):
        halo_copy(core, near * nb + j, partner).start()
        extra_copy(j).start()

    for copy in load(core):
        copy.wait()
    products(core)

    for copy in constants:
        copy.wait()
    prev_kg[0] = prev_ref[...] * jnp.where(c > 0, 1.0, 0.0).astype(bf16)
    prev_kg[1] = prev_ref[...] * jnp.where(c < nc - 1, -1.0, 0.0).astype(bf16)

    def forward(matrix, value):
        return jnp.dot(
            matrix, jnp.concatenate([value, value], axis=0), preferred_element_type=f32
        )

    def own_spectra(s):
        def step(j, carry):
            b = s * nb + j
            spec[0, b] = forward(own_ref[...], kg[0, b])
            spec[1, b] = forward(own_ref[...], kg[1, b])
            return carry

        lax.fori_loop(0, nb, step, 0)

    def tap_spectra(s):
        def step(j, carry):
            b = s * nb + j
            taps = h_ref[:, pl.ds(pl.multiple_of(b * W, W), W)]
            spec_h[b] = forward(own_ref[...], taps)
            return carry

        lax.fori_loop(0, nb, step, 0)

    own_spectra(core)

    def times(a, b):
        ar, ai, br, bi = a[:F], a[F:], b[:F], b[F:]
        return ar * br - ai * bi, ar * bi + ai * br

    def times_conj(a, b):
        ar, ai, br, bi = a[:F], a[F:], b[:F], b[F:]
        return ar * br + ai * bi, ai * br - ar * bi

    def inverse(re, im):
        value = jnp.concatenate([re, im], axis=0)
        hi = value.astype(bf16)
        lo = (value - hi.astype(f32)).astype(bf16)
        return jnp.dot(
            back_ref[...], jnp.concatenate([hi, lo, hi], axis=0), preferred_element_type=f32
        )

    first = core == 0

    def early_terms(j, carry):
        b = core * nb + j
        halo_copy(1 - core, b, partner).wait_recv()
        extra_copy(j).wait_recv()
        fast = forward(prev_kg[near], halo[near, b])
        other = forward(prev_ref[...], extra[j])
        own_k = spec[0, b]
        own_g = spec[1, b]
        spec[near, b] = spec[near, b] + fast
        re0, im0 = times_conj(jnp.where(first, own_g + fast, own_g), jnp.where(first, own_k, own_k + fast))
        re1, im1 = times_conj(jnp.where(first, -fast, other), jnp.where(first, other, fast))
        mates[j] = jnp.where(first, own_g, own_k)
        early_sum[j, :F] = re0 + re1
        early_sum[j, F:] = im0 + im1
        return carry

    lax.fori_loop(0, nb, early_terms, 0)

    def gradient(j, carry):
        b = core * nb + j
        halo_copy(core, b, partner).wait_recv()
        slow = forward(prev_kg[core], halo[core, b])
        mate = mates[j]
        re, im = times_conj(jnp.where(first, mate, slow), jnp.where(first, slow, mate))
        value = inverse(early_sum[j, :F] + re, early_sum[j, F:] + im)
        part_x[j] = jnp.transpose(value).astype(bf16).reshape(NX, W // NX, T)
        for d in (2, 1, 3):
            pltpu.make_async_remote_copy(
                src_ref=part_x.at[j, lax.rem(x + d, NX)], dst_ref=recv_x.at[j, d - 1],
                send_sem=send_x, recv_sem=sem_x.at[j], device_id=at_x(d), device_id_type=MESH,
            ).start()
        spec[core, b] = spec[core, b] + slow
        return carry

    lax.fori_loop(0, nb, gradient, 0, unroll=True)
    @pl.when(turn)
    def _():
        send_late(0, nb // 2)


    def outputs(s, first_block, last_block):
        def step(j, carry):
            b = s * nb + j
            if s is near:
                late_copy(0, b, right).wait_recv()
                late_copy(1, b, left).wait_recv()
            k_all = spec[0, b]
            g_all = spec[1, b]
            if s is near:
                k_all += forward(prev_kg[0], halo[0, b])
                g_all += forward(prev_kg[1], halo[1, b])
            taps = spec_h[b]
            cols = pl.ds(pl.multiple_of(j * W, W), W)
            full = pl.ds(pl.multiple_of(b * W, W), W)
            m = inverse(*times(k_all, taps))
            y_hbm[0, :, full] = (q_ref[s, :, cols].astype(f32) * m).astype(bf16)
            gq_hbm[0, :, full] = (g_ref[s, :, cols].astype(f32) * m).astype(bf16)
            m = inverse(*times_conj(g_all, taps))
            gk_hbm[0, :, full] = (v_ref[s, :, cols].astype(f32) * m).astype(bf16)
            gv_hbm[0, :, full] = (k_ref[s, :, cols].astype(f32) * m).astype(bf16)
            return carry

        lax.fori_loop(first_block, last_block, step, 0)

    def landed(ref, sem):
        pltpu.make_async_copy(ref, ref, sem).wait()

    own_spectra(near)

    for j in range(nb):
        landed(recv_x.at[j], sem_x.at[j])
        total = part_x[j, x].astype(f32)
        for d in range(NX - 1):
            total += recv_x[j, d].astype(f32)
        part_y[j] = total.astype(bf16).reshape(2, W // NX // 2, T)
        for core_to in range(2):
            mine = jnp.logical_and(jnp.logical_and(own_source, yy == core * nb + j), core == core_to)

            @pl.when(jnp.logical_not(mine))
            def _():
                pltpu.make_async_remote_copy(
                    src_ref=part_y.at[j, core_to], dst_ref=recv_y.at[yy],
                    send_sem=send_y, recv_sem=sem_y.at[yy],
                    device_id=at(core * nb + j, x, core_to), device_id_type=MESH,
                ).start()

            @pl.when(mine)
            def _():
                recv_y[yy] = part_y[j, core_to]

    send_near()
    @pl.when(jnp.logical_not(turn))
    def _():
        send_late(0, nb)

    tap_spectra(core)
    tap_spectra(near)
    outputs(core, 0, nb)

    @pl.when(turn)
    def _():
        send_late(nb // 2, nb)


    for ys in range(ny):
        @pl.when(jnp.logical_not(jnp.logical_and(ys == yy, own_source)))
        def _():
            landed(recv_y.at[ys], sem_y.at[ys])
    total = recv_y[0].astype(f32)
    for ys in range(1, ny):
        total += recv_y[ys].astype(f32)
    part_z[...] = total.astype(bf16)
    for d in sorted(range(1, nz), key=lambda d: abs(d - nz // 2)):
        pltpu.make_async_remote_copy(
            src_ref=part_z, dst_ref=recv_z.at[d - 1], send_sem=send_z, recv_sem=sem_z,
            device_id=at_z(d), device_id_type=MESH,
        ).start()

    outputs(near, 0, nb)

    landed(kg.at[0], halo_send.at[0])
    landed(kg.at[1], halo_send.at[1])
    landed(extra, extra_send)
    landed(recv_x, send_x)
    landed(recv_y.at[pl.ds(0, ny - 1)], send_y)

    @pl.when(jnp.logical_not(own_source))
    def _():
        landed(recv_y.at[ny - 1], send_y)

    landed(recv_z, sem_z)
    total = part_z[...].astype(f32)
    for d in range(nz - 1):
        total += recv_z[d].astype(f32)
    gf_ref[...] = total * (1.0 / math.sqrt(T * nc * nz))

    landed(recv_z, send_z)


def write_out(*refs):
    sem = refs[10]
    copies = [pltpu.make_async_copy(refs[i], refs[5 + i], sem.at[i]) for i in range(5)]
    for copy in copies:
        copy.start()
    for copy in copies:
        copy.wait()


def per_device(query_act, key_act, value_act, grad_out, filter_taps):
    channels = filter_taps.shape[1]
    ny = channels // W
    nz = lax.axis_size("dp")
    own, prev, back = transforms()
    big = jax.ShapeDtypeStruct((1, T, channels), bf16)
    half = channels // 2
    cols = W // NX // 2
    small = jax.ShapeDtypeStruct((cols, T), f32)
    hbm = pl.BlockSpec(memory_space=pl.ANY)
    vmem = pl.BlockSpec(memory_space=pltpu.VMEM)
    dma = pltpu.SemaphoreType.DMA
    limit = VMEM_BYTES
    outs = pl.pallas_call(
        functools.partial(kernel, nz, ny),
        out_shape=[pltpu.VMEM(big.shape, bf16)] * 4 + [pltpu.VMEM(small.shape, f32)],
        in_specs=[hbm] * 8,
        out_specs=[vmem] * 5,
        scratch_shapes=[
            *[pltpu.VMEM((2, T, half), bf16)] * 4,
            pltpu.VMEM((T, channels), bf16),
            pltpu.VMEM((2 * F, 2 * T), bf16),
            pltpu.VMEM((2 * F, 2 * T), bf16),
            pltpu.VMEM((T, 6 * F), bf16),
            pltpu.VMEM((2, 2 * F, 2 * T), bf16),
            pltpu.VMEM((2, ny, T, W), bf16),
            pltpu.VMEM((2, ny, T, W), bf16),
            pltpu.VMEM((ny // 2, T, W), bf16),
            pltpu.VMEM((2, ny, 2 * F, W), f32),
            pltpu.VMEM((ny, 2 * F, W), f32),
            pltpu.VMEM((ny // 2, 2 * F, W), f32),
            pltpu.VMEM((ny // 2, 2 * F, W), f32),
            pltpu.VMEM((ny // 2, NX, W // NX, T), bf16),
            pltpu.VMEM((ny // 2, NX - 1, W // NX, T), bf16),
            pltpu.VMEM((ny // 2, 2, cols, T), bf16),
            pltpu.VMEM((ny, cols, T), bf16),
            pltpu.VMEM((cols, T), bf16),
            pltpu.VMEM((nz - 1, cols, T), bf16),
            dma((2, 4)), dma((4,)), dma((2,)), dma((2, ny // 2)), dma((2, ny // 2)),
            dma(()), dma((ny // 2,)), dma(()), dma((ny // 2,)), dma(()), dma((ny,)), dma(()), dma(()),
        ],
        compiler_params=pltpu.CompilerParams(
            collective_id=1, has_side_effects=True, vmem_limit_bytes=limit
        ),
    )(query_act, key_act, value_act, grad_out, filter_taps, own, prev, back)
    *done, summed = pl.pallas_call(
        write_out,
        out_shape=[big] * 4 + [small],
        in_specs=[vmem] * 5,
        out_specs=[hbm] * 5,
        scratch_shapes=[dma((5,))],
        compiler_params=pltpu.CompilerParams(vmem_limit_bytes=2**20),
    )(*outs)
    return (*done, summed.T)


def solution(mesh):
    spread = P("dp", "ctx", None)
    return jax.shard_map(
        per_device, mesh=mesh, in_specs=(spread,) * 4 + (P(),),
        out_specs=(spread,) * 4 + (P(None, "ctx"),), check_vma=False,
    )
```
